256 devices in a mesh: dp: 32 (over z, y), seq: 8 (over x, core).
Axes of the slice: x: 4, y: 4, z: 8, core: 2. Of those that a mesh axis runs over, the one named last changes fastest.
Arguments:
- latent_codes: bfloat16 [32, 8, 20, 256], P('dp', 'seq'), may hold values from -4 to 4
- latent_scales: bfloat16 [32, 8, 20, 64], P('dp', 'seq'), may hold values from 0.099609375 to 2
- send_list: int32 [32, 8, 32], P('dp', 'seq'), may hold values from -1 to 19, as said below
- embed_weight: bfloat16 [64, 3072], replicated, may hold values from -0.75 to 0.75
- modulation_offset: float32 [32, 3072], P('dp'), may hold values from -3 to 3
- mod_scale: float32 [32, 3072], P('dp'), may hold values from -0.9 to 0.9
- qkv_weight: bfloat16 [3072, 6144], P('dp', 'seq'), may hold values from -0.109375 to 0.109375
- text_qkv: bfloat16 [32, 128, 6144], P('dp', 'seq'), may hold values from -8 to 8
- text_len: int32 [32], P('dp'), may hold values from 32 to 128, as said below
- out_grad_img: bfloat16 [32, 1024, 2048], P('dp', 'seq'), may hold values from -6 to 6
- out_grad_txt: bfloat16 [32, 128, 2048], P('dp', 'seq'), may hold values from -6 to 6
Outputs:
- img_attn: bfloat16 [32, 1024, 2048], P('dp', 'seq')
- txt_attn: bfloat16 [32, 128, 2048], P('dp', 'seq')
- code_grad: float32 [32, 8, 20, 256], P('dp', 'seq')
- embed_grad: float32 [64, 3072], replicated
The draws below stay inside these ranges and needn't reach their ends.
Inputs may be any that keep to these rules, and one draw needn't show every extreme that they name: `send_list`: -1 means no block; on each device every one of its 20 blocks goes to exactly one destination sample, so a device sends at most one block to each sample. `text_len`: some sample has all 128 text tokens valid.
All inputs are finite; a program needn't handle non-finite values.
Results may differ from the reference program's by a relative error of at most 0.025.
Values may be sent and summed in bfloat16 or wider, within the bound.
A program may use at most 128 MiB of HBM per device.

```python
import math
import jax
import jax.numpy as jnp
from jax import lax

D = 3072
HEADS = 16
HD = 128
CH = 64
BLK = 4
LOCAL = 20
IMGLEN = 1024
TXT = 128
N_DP = 32
N_SEQ = 8


def draw_send_list(key, part):
    key = jax.random.fold_in(key, 11)
    keys = jax.random.split(key, N_DP * N_SEQ)
    perms = jax.vmap(lambda single: jax.random.permutation(single, N_DP))(keys)
    ranks = jnp.argsort(perms, axis=1)
    lists = jnp.where(ranks < LOCAL, ranks, -1).astype(jnp.int32)
    return lists.reshape(N_DP, N_SEQ, N_DP)


def draw_text_len(key, part):
    key = jax.random.fold_in(key, 7)
    first, second = jax.random.split(key)
    lengths = jax.random.randint(first, (N_DP,), TXT // 4, TXT + 1)
    order = jax.random.permutation(second, N_DP)
    lengths = lengths.at[order[0]].set(TXT).at[order[1]].set(TXT // 4)
    return lengths.astype(jnp.int32)


def draw_text_qkv(key, part):
    key = jax.random.fold_in(key, 5)
    first = jax.random.fold_in(key, 0)
    values = jnp.clip(jax.random.normal(first, (N_DP, TXT, HEADS, 3, HD), jnp.float32), -4.0, 4.0)
    return values.reshape(N_DP, TXT, HEADS * 3 * HD).astype(jnp.bfloat16)


def levels(key, dims, shards, low, high):
    loudness, own = 1.0, jax.random.fold_in(key, 6)
    for dim, shards_of in shards:
        draws = jnp.exp(jax.random.uniform(jax.random.fold_in(own, dim), (shards_of,), jnp.float32, low / len(shards), high / len(shards)))
        loudness = loudness * jnp.repeat(draws, dims[dim] // shards_of).reshape([-1 if axis == dim else 1 for axis in range(len(dims))])
    return loudness


def scatter_about(key, dims, width, most, shards=(), kind=jnp.bfloat16):
    level = levels(key, dims, shards, -0.22, 0.18) if shards else 1.0
    result = jax.random.normal(key, dims, jnp.float32) * width * level
    return jnp.minimum(jnp.maximum(result, -most), most).astype(kind)


def setup_inputs(seed: int = 0) -> dict:
    seeds = jax.random.split(jax.random.key(seed), 12)
    latent_codes = scatter_about(seeds[0], (N_DP, N_SEQ, LOCAL, BLK * CH), 1.0, 4.0, ((0, 32), (1, 8)))
    latent_scales = jnp.clip(jnp.exp(math.log(2.0) - 2.9996462 * jax.random.uniform(seeds[1], (N_DP, N_SEQ, LOCAL, CH), jnp.float32) ** levels(seeds[1], (N_DP, N_SEQ, LOCAL, CH), ((0, 32), (1, 8)), -0.2, 0.2)), 0.099609375, 2.0).astype(jnp.bfloat16)
    send_list = draw_send_list(jax.random.fold_in(seeds[11], 71), 0)
    embed_weight = scatter_about(seeds[3], (CH, D), CH ** -0.5, 0.75)
    modulation_offset = scatter_about(seeds[4], (N_DP, D), 0.5, 3.0, ((0, 32),), jnp.float32)
    mod_scale = scatter_about(seeds[5], (N_DP, D), 0.3, 0.9, ((0, 32),), jnp.float32)
    qkv_weight = scatter_about(seeds[6], (D, HEADS * 3 * HD), D ** -0.5, 0.109375, ((0, 32), (1, 8)))
    text_qkv = draw_text_qkv(jax.random.fold_in(seeds[11], 71), 0)
    text_len = draw_text_len(jax.random.fold_in(seeds[11], 71), 0)
    out_grad_img = scatter_about(seeds[9], (N_DP, IMGLEN, HEADS * HD), 1.0, 6.0, ((0, 32), (1, 8)))
    out_grad_txt = scatter_about(seeds[10], (N_DP, TXT, HEADS * HD), 1.0, 6.0, ((0, 32), (1, 8)))
    return dict(latent_codes=latent_codes, latent_scales=latent_scales, send_list=send_list, embed_weight=embed_weight, modulation_offset=modulation_offset, mod_scale=mod_scale, qkv_weight=qkv_weight, text_qkv=text_qkv, text_len=text_len, out_grad_img=out_grad_img, out_grad_txt=out_grad_txt)


eps = 1e-06

def layer_normalize(x):
    row_average = lax.optimization_barrier(jnp.mean(x, axis=-1, keepdims=True))
    centred = x - row_average
    inverse_deviation = lax.rsqrt(lax.optimization_barrier(jnp.mean(centred * centred, axis=-1, keepdims=True)) + eps)
    return (centred * inverse_deviation, inverse_deviation)

def norm_backward_rule(upstream_gradient, centred_normalized, inverse_deviation, scale_factor):
    gradient_values = upstream_gradient * (1.0 + scale_factor)
    gradient_average = lax.optimization_barrier(jnp.mean(gradient_values, axis=-1, keepdims=True))
    gradient_input_average = lax.optimization_barrier(jnp.mean(gradient_values * centred_normalized, axis=-1, keepdims=True))
    return inverse_deviation * (gradient_values - gradient_average - centred_normalized * gradient_input_average)

def attend(query, keys, values, dout, key_ok, query_ok):
    factor = 1.0 / jnp.sqrt(jnp.float32(query.shape[-1]))
    qf = query.astype(jnp.float32)
    kf = keys.astype(jnp.float32)
    vf = values.astype(jnp.float32)
    score = jnp.einsum('qhd,khd->hqk', qf, kf) * factor
    score = jnp.where(key_ok[None, None, :], score, jnp.float32(-1e+30))
    top = lax.optimization_barrier(jnp.max(score, axis=-1, keepdims=True))
    expo = jnp.where(key_ok[None, None, :], jnp.exp(score - top), jnp.float32(0.0))
    prob = (expo / lax.optimization_barrier(jnp.sum(expo, axis=-1, keepdims=True))).astype(jnp.bfloat16)
    pf = prob.astype(jnp.float32)
    out = jnp.einsum('hqk,khd->qhd', pf, vf)
    out = jnp.where(query_ok[:, None, None], out, jnp.float32(0.0)).astype(jnp.bfloat16)
    dmask = jnp.where(query_ok[:, None, None], dout, jnp.zeros_like(dout)).astype(jnp.float32)
    delta = jnp.transpose(lax.optimization_barrier(jnp.sum(dmask * out.astype(jnp.float32), axis=-1)), (1, 0))
    dprob = jnp.einsum('qhd,khd->hqk', dmask, vf)
    dscore = (pf * (dprob - delta[:, :, None])).astype(jnp.bfloat16).astype(jnp.float32)
    dquery = (jnp.einsum('hqk,khd->qhd', dscore, kf) * factor).astype(jnp.bfloat16)
    dkey = (jnp.einsum('hqk,qhd->khd', dscore, qf) * factor).astype(jnp.bfloat16)
    dvalue = jnp.einsum('hqk,qhd->khd', pf, dmask).astype(jnp.bfloat16)
    return (out, dquery, dkey, dvalue)

def reference(latent_codes, latent_scales, send_list, embed_weight, modulation_offset, mod_scale, qkv_weight, text_qkv, text_len, out_grad_img, out_grad_txt):

    def one_sample(sample_index):
        index = send_list[:, :, sample_index]
        used = index >= 0
        pick = jnp.maximum(index, 0).astype(jnp.int32)
        codes = jnp.take_along_axis(latent_codes, pick[:, :, None, None], axis=2)[:, :, 0]
        scl = jnp.take_along_axis(latent_scales, pick[:, :, None, None], axis=2)[:, :, 0]
        codes = jnp.where(used[:, :, None], codes.astype(jnp.float32), jnp.float32(0.0))
        scl = jnp.where(used[:, :, None], scl.astype(jnp.float32), jnp.float32(0.0))
        deq = (codes.reshape(N_DP, N_SEQ, BLK, CH) * scl[:, :, None, :]).astype(jnp.bfloat16)
        deq = jnp.transpose(deq, (1, 0, 2, 3)).reshape(IMGLEN, CH)
        live = jnp.repeat(jnp.transpose(used, (1, 0)).reshape(N_SEQ * N_DP), BLK)
        input_values = jnp.dot(deq, embed_weight, preferred_element_type=jnp.float32)
        centred_normalized, inverse_deviation = layer_normalize(input_values)
        scale_factor = mod_scale[sample_index]
        normalized_rows = (centred_normalized * (1.0 + scale_factor) + modulation_offset[sample_index]).astype(jnp.bfloat16)
        qkv = jnp.dot(normalized_rows, qkv_weight, preferred_element_type=jnp.float32).astype(jnp.bfloat16)
        joint = jnp.concatenate([text_qkv[sample_index], qkv], axis=0).reshape(TXT + IMGLEN, HEADS, 3, HD)
        text_ok = jnp.arange(TXT) < text_len[sample_index]
        valid = jnp.concatenate([text_ok, live])
        dout = jnp.concatenate([out_grad_txt[sample_index], out_grad_img[sample_index]], axis=0).reshape(TXT + IMGLEN, HEADS, HD)
        out, dquery, dkey, dvalue = attend(joint[:, :, 0], joint[:, :, 1], joint[:, :, 2], dout, valid, valid)
        dimg = jnp.stack([dquery, dkey, dvalue], axis=2)[TXT:].reshape(IMGLEN, HEADS * 3 * HD)
        normalized_gradient = jnp.dot(dimg, qkv_weight.T, preferred_element_type=jnp.float32)
        input_gradient_values = norm_backward_rule(normalized_gradient, centred_normalized, inverse_deviation, scale_factor)
        input_gradient_narrow = input_gradient_values.astype(jnp.bfloat16)
        ddeq = jnp.dot(input_gradient_narrow, embed_weight.T, preferred_element_type=jnp.float32)
        dweight = jnp.dot(deq.T, input_gradient_narrow, preferred_element_type=jnp.float32)
        flat = out.reshape(TXT + IMGLEN, HEADS * HD)
        return (flat[TXT:], flat[:TXT], ddeq.reshape(N_SEQ, N_DP, BLK * CH), dweight)
    img_attn, txt_attn, ddeq_all, dweights = lax.map(one_sample, jnp.arange(N_DP))
    embed_grad = lax.optimization_barrier(jnp.sum(dweights, axis=0))
    onehot = (send_list[:, :, None, :] == jnp.arange(LOCAL)[None, None, :, None]).astype(jnp.float32)
    summed = jnp.einsum('esbd,dser->esbr', onehot, ddeq_all, precision=lax.Precision.HIGHEST)
    code_grad = (summed.reshape(N_DP, N_SEQ, LOCAL, BLK, CH) * latent_scales.astype(jnp.float32)[:, :, :, None, :]).reshape(N_DP, N_SEQ, LOCAL, BLK * CH)
    return (img_attn, txt_attn, code_grad, embed_grad)
```

```python
import jax
import jax.numpy as jnp
from jax import lax
from jax.sharding import PartitionSpec as P

HD = 128


eps = 1e-06


def layer_normalize(x):
    row_average = jnp.mean(x, axis=-1, keepdims=True)
    centred = x - row_average
    inverse_deviation = lax.rsqrt(jnp.mean(centred * centred, axis=-1, keepdims=True) + eps)
    return (centred * inverse_deviation, inverse_deviation)


def attend(query, keys, values, dout, key_ok, query_ok):
    factor = 1.0 / jnp.sqrt(jnp.float32(query.shape[-1]))
    score = jnp.einsum("qhd,khd->hqk", query, keys, preferred_element_type=jnp.float32) * factor
    score = jnp.where(key_ok[None, None, :], score, jnp.float32(-1e30))
    top = jnp.max(score, axis=-1, keepdims=True)
    expo = jnp.where(key_ok[None, None, :], jnp.exp(score - top), jnp.float32(0.0))
    prob = (expo / jnp.sum(expo, axis=-1, keepdims=True)).astype(jnp.bfloat16)
    out = jnp.einsum("hqk,khd->qhd", prob, values, preferred_element_type=jnp.float32)
    out = jnp.where(query_ok[:, None, None], out, jnp.float32(0.0)).astype(jnp.bfloat16)
    dmask = jnp.where(query_ok[:, None, None], dout, jnp.zeros_like(dout))
    delta = jnp.transpose(
        jnp.sum(dmask.astype(jnp.float32) * out.astype(jnp.float32), axis=-1), (1, 0)
    )
    dprob = jnp.einsum("qhd,khd->hqk", dmask, values, preferred_element_type=jnp.float32)
    dscore = (prob.astype(jnp.float32) * (dprob - delta[:, :, None])).astype(jnp.bfloat16)
    dquery = (
        jnp.einsum("hqk,khd->qhd", dscore, keys, preferred_element_type=jnp.float32) * factor
    ).astype(jnp.bfloat16)
    dkey = (
        jnp.einsum("hqk,qhd->khd", dscore, query, preferred_element_type=jnp.float32) * factor
    ).astype(jnp.bfloat16)
    dvalue = jnp.einsum("hqk,qhd->khd", prob, dmask, preferred_element_type=jnp.float32).astype(
        jnp.bfloat16
    )
    return (out, dquery, dkey, dvalue)


def split2(value):
    high = value.astype(jnp.bfloat16)
    low = (value - high.astype(jnp.float32)).astype(jnp.bfloat16)
    return jnp.concatenate([high, low], axis=0)


def per_device(
    latent_codes,
    latent_scales,
    send_list,
    embed_weight,
    modulation_offset,
    mod_scale,
    qkv_weight,
    text_qkv,
    text_len,
    out_grad_img,
    out_grad_txt,
):
    peers = lax.axis_size("dp")
    codes = latent_codes[0, 0]
    scales = latent_scales[0, 0]
    slots = send_list[0, 0]
    channels = scales.shape[1]
    block_len = codes.shape[1] // channels
    local_count = codes.shape[0]
    used = slots >= 0
    pick = jnp.maximum(slots, 0)
    out_codes = jnp.where(used[:, None], jnp.take(codes, pick, axis=0), jnp.zeros((), jnp.bfloat16))
    out_scales = jnp.where(
        used[:, None], jnp.take(scales, pick, axis=0), jnp.zeros((), jnp.bfloat16)
    )
    got_codes, got_scales = (
        lax.all_to_all(out_codes, "dp", split_axis=0, concat_axis=0, tiled=True),
        lax.all_to_all(out_scales, "dp", split_axis=0, concat_axis=0, tiled=True),
    )
    got_f = got_scales.astype(jnp.float32)
    deq = (
        (got_codes.astype(jnp.float32).reshape(peers, block_len, channels) * got_f[:, None, :])
        .astype(jnp.bfloat16)
        .reshape(peers, block_len * channels)
    )
    live = (jnp.sum(got_f, axis=1) > 0).astype(jnp.bfloat16)
    shift_offset = modulation_offset[0]
    scale_factor = mod_scale[0]
    tokens = deq.reshape(-1, channels)
    width = embed_weight.shape[1]
    input_values = jnp.dot(tokens, embed_weight, preferred_element_type=jnp.float32)
    centred_normalized, inverse_deviation = layer_normalize(input_values)
    embed_f = embed_weight.astype(jnp.float32)
    embed_centred = embed_f - jnp.mean(embed_f, axis=1, keepdims=True)
    packed = jnp.concatenate(
        [tokens.astype(jnp.float32), inverse_deviation, jnp.repeat(live, block_len)[:, None].astype(jnp.float32)],
        axis=1,
    )
    packed_all = lax.all_gather(packed, "seq", axis=0, tiled=True)
    tokens_all = packed_all[:, :channels].astype(jnp.bfloat16)
    inv_all = packed_all[:, channels : channels + 1]
    live_all = packed_all[:, channels + 1]
    image_count = packed_all.shape[0]
    qkv_width = qkv_weight.shape[1]
    weight = lax.all_gather(qkv_weight, "dp", axis=0, tiled=True)
    modulated = split2(jnp.concatenate([embed_centred * (1.0 + scale_factor), shift_offset[None]], axis=0))
    product = jnp.dot(modulated, weight, preferred_element_type=jnp.float32)
    product = product[: channels + 1] + product[channels + 1 :]
    mixed, constant = product[:channels], product[channels:]
    mixed2 = split2(mixed)
    qkv_img = (
        jnp.dot(
            jnp.concatenate([tokens_all, tokens_all], axis=1), mixed2, preferred_element_type=jnp.float32
        )
        * inv_all
        + constant
    ).astype(jnp.bfloat16)
    text_heads, grad_img, grad_txt = (
        lax.all_to_all(text_qkv[0], "seq", split_axis=1, concat_axis=0, tiled=True),
        lax.all_to_all(out_grad_img[0], "seq", split_axis=1, concat_axis=0, tiled=True),
        lax.all_to_all(out_grad_txt[0], "seq", split_axis=1, concat_axis=0, tiled=True),
    )
    heads_dev = qkv_width // (3 * HD)
    text_count = text_heads.shape[0]
    total = text_count + image_count
    joint = jnp.concatenate([text_heads, qkv_img], axis=0).reshape(total, heads_dev, 3, HD)
    text_ok = jnp.arange(text_count) < text_len[0]
    img_ok = live_all > 0
    valid = jnp.concatenate([text_ok, img_ok])
    dout = jnp.concatenate([grad_txt, grad_img], axis=0).reshape(total, heads_dev, HD)
    out, dquery, dkey, dvalue = attend(
        joint[:, :, 0], joint[:, :, 1], joint[:, :, 2], dout, valid, valid
    )
    flat = out.reshape(total, heads_dev * HD)
    res_img, res_txt = (
        lax.all_to_all(flat[text_count:], "seq", split_axis=0, concat_axis=1, tiled=True),
        lax.all_to_all(flat[:text_count], "seq", split_axis=0, concat_axis=1, tiled=True),
    )
    dimg = jnp.stack([dquery, dkey, dvalue], axis=2)[text_count:].reshape(image_count, qkv_width)
    grad_part = lax.dot_general(
        dimg, mixed2[:channels], (((1,), (1,)), ((), ())), preferred_element_type=jnp.float32
    )
    scaled = tokens_all.astype(jnp.float32) * inv_all
    project = jnp.sum(scaled * grad_part, axis=1, keepdims=True) * (1.0 / width)
    gram = lax.dot_general(
        (scaled * inv_all * project).astype(jnp.bfloat16),
        tokens_all,
        (((0,), (0,)), ((), ())),
        preferred_element_type=jnp.float32,
    )
    seen = lax.dot_general(
        scaled.astype(jnp.bfloat16), dimg, (((0,), (0,)), ((), ())), preferred_element_type=jnp.float32
    ).astype(jnp.bfloat16)
    dweight = lax.dot_general(
        seen, weight, (((1,), (1,)), ((), ())), preferred_element_type=jnp.float32
    ) * (1.0 + scale_factor)
    dweight = dweight - jnp.mean(dweight, axis=1, keepdims=True)
    dweight = dweight - jnp.dot(gram.astype(jnp.bfloat16), embed_centred.astype(jnp.bfloat16), preferred_element_type=jnp.float32)
    members = lax.axis_size("seq")
    part = lax.all_to_all(
        dweight.reshape(channels, members, width // members).astype(jnp.bfloat16), "seq", split_axis=1, concat_axis=1, tiled=True
    )
    part = jnp.sum(part.astype(jnp.float32), axis=1)
    part = lax.all_to_all(
        part.reshape(peers, -1), "dp", split_axis=0, concat_axis=0, tiled=True
    )
    part = jnp.sum(part, axis=0)
    part = lax.all_gather(part, "dp", axis=0, tiled=True).reshape(channels, width // members)
    embed_grad = lax.all_gather(part, "seq", axis=1, tiled=True)
    grad_own = jnp.sum(
        lax.all_to_all(
            grad_part.reshape(members, -1, channels).astype(jnp.bfloat16), "seq", split_axis=0, concat_axis=0, tiled=True
        ).astype(jnp.float32),
        axis=0,
    )
    project_own = (
        jnp.sum(tokens.astype(jnp.float32) * grad_own, axis=1, keepdims=True) * inverse_deviation * (1.0 / width)
    )
    back = lax.dot_general(
        centred_normalized.astype(jnp.bfloat16),
        embed_weight,
        (((1,), (1,)), ((), ())),
        preferred_element_type=jnp.float32,
    )
    ddeq = inverse_deviation * (grad_own - back * project_own)
    returned = lax.all_to_all(
        ddeq.reshape(peers, block_len * channels).astype(jnp.bfloat16),
        "dp",
        split_axis=0,
        concat_axis=0,
        tiled=True,
    ).astype(jnp.float32)
    onehot = (slots[None, :] == jnp.arange(local_count)[:, None]).astype(jnp.float32)
    summed = jnp.dot(onehot, returned, precision=lax.Precision.HIGHEST)
    code_grad = (
        summed.reshape(local_count, block_len, channels) * scales.astype(jnp.float32)[:, None, :]
    ).reshape(local_count, block_len * channels)
    return (res_img[None], res_txt[None], code_grad[None, None], embed_grad)


def solution(mesh):
    return jax.shard_map(
        per_device,
        mesh=mesh,
        in_specs=(
            P("dp", "seq", None, None),
            P("dp", "seq", None, None),
            P("dp", "seq", None),
            P(),
            P("dp", None),
            P("dp", None),
            P("dp", "seq"),
            P("dp", "seq", None),
            P("dp"),
            P("dp", "seq", None),
            P("dp", "seq", None),
        ),
        out_specs=(P("dp", "seq", None), P("dp", "seq", None), P("dp", "seq", None, None), P()),
        check_vma=False,
    )
```

```python
import functools
import math

import jax
import jax.numpy as jnp
from jax import lax
from jax.experimental import pallas as pl
from jax.experimental.pallas import tpu as pltpu
from jax.sharding import PartitionSpec as P

MESH = pl.DeviceIdType.MESH
BF, F32 = jnp.bfloat16, jnp.float32
HD = 128
LANES = 128
EPS = 1e-06
Y = 4
CORES = 2
HALF = Y // CORES
LIVE, INV_HIGH, INV_LOW, TEXT_LEN = 64, 65, 66, 67


def mm(a, b):
    return jnp.dot(a, b, preferred_element_type=F32)


def mm_nt(a, b):
    return lax.dot_general(a, b, (((1,), (1,)), ((), ())), preferred_element_type=F32)


def mm_tn(a, b):
    return lax.dot_general(a, b, (((0,), (0,)), ((), ())), preferred_element_type=F32)


def iota(shape, dim):
    return lax.broadcasted_iota(jnp.int32, shape, dim)


def over(value, power):
    return lax.shift_right_logical(value, jnp.full_like(value, power.bit_length() - 1))


def within(value, power):
    return jnp.bitwise_and(value, power - 1)


def split(value):
    high = value.astype(BF)
    return high, (value - high.astype(F32)).astype(BF)


def kernel(
    n_dp,
    n_seq,
    text_len,
    codes,
    scales,
    slot_col,
    slot_row,
    embed,
    shift,
    scale,
    weight,
    text,
    grad_img,
    grad_txt,
    out_img,
    out_txt,
    code_out,
    embed_out,
    a_send,
    a_recv,
    own_tok,
    own_mods,
    tok,
    mods,
    wbuf,
    amat,
    mixed,
    const,
    qkv,
    dout,
    kaug,
    vaug,
    kt,
    vt,
    dot_t,
    valid_row,
    dk_acc,
    dv_acc,
    out_buf,
    dqkv,
    f_send,
    f_recv,
    back,
    g_send,
    g_recv,
    t_send,
    h1,
    h2,
    h3,
    send,
    recv,
    mod_send,
    ring_right,
    ring_left,
    ring_send,
):
    d, j = lax.axis_index("dp"), lax.axis_index("seq")
    z, y = lax.div(d, Y), lax.rem(d, Y)
    x, c = lax.div(j, CORES), lax.rem(j, CORES)
    slot, core = lax.rem(y, HALF), lax.div(y, HALF)
    own = core == c
    head = Y * x + y
    n_z, heads = n_dp // Y, Y * n_seq // CORES
    channels, width = embed.shape
    rows = weight.shape[0]
    local = grad_img.shape[0]
    tloc = grad_txt.shape[0]
    images, texts = local * n_seq, tloc * n_seq
    total = images + texts
    block = local // n_dp
    cols = 3 * HD

    def same(dp, seq):
        return jnp.logical_and(dp == d, seq == j)

    def remote(src, dst, k, dp, seq):
        pltpu.make_async_remote_copy(
            src_ref=src,
            dst_ref=dst,
            send_sem=send.at[k],
            recv_sem=recv.at[k],
            device_id=(dp, seq),
            device_id_type=MESH,
        ).start()

    def push(src, dst, k, dp, seq):
        @pl.when(same(dp, seq))
        def _():
            pltpu.make_async_copy(src, dst, recv.at[k]).start()

        @pl.when(jnp.logical_not(same(dp, seq)))
        def _():
            remote(src, dst, k, dp, seq)

    def arrived(ref, k):
        pltpu.make_async_copy(ref, ref, recv.at[k]).wait()

    def left_here(ref, k):
        pltpu.make_async_copy(ref, ref, send.at[k]).wait()

    def sent(some, whole, k):
        @pl.when(own)
        def _():
            left_here(some, k)

        @pl.when(jnp.logical_not(own))
        def _():
            left_here(whole, k)

    A, WY, MOD, TXT, DIMG, TOK, SIB, OIMG, OTXT, FEAT, G, H1, H2, H3, DTXT = range(15)

    def plane_peer(i):
        py = lax.rem(y + lax.div(i, n_seq), Y)
        return py, lax.rem(j + lax.rem(i, n_seq), n_seq)

    barrier = pltpu.get_barrier_semaphore()

    def greet_dp(i, carry):
        pl.semaphore_signal(
            barrier, inc=1, device_id=(lax.rem(d + i, n_dp), j), device_id_type=MESH
        )
        return carry

    lax.fori_loop(1, n_dp, greet_dp, 0)

    def greet_plane(i, carry):
        py = lax.rem(y + lax.div(i, n_seq - 1), Y)
        pj = lax.rem(j + 1 + lax.rem(i, n_seq - 1), n_seq)
        pl.semaphore_signal(barrier, inc=1, device_id=(z * Y + py, pj), device_id_type=MESH)
        return carry

    lax.fori_loop(0, Y * (n_seq - 1), greet_plane, 0)

    pick = (slot_col[...] == iota((n_dp, codes.shape[0]), 1)).astype(F32).astype(BF)
    used = jnp.sum(pick.astype(F32), axis=1, keepdims=True)
    pad_eye = (iota((channels, LANES), 0) == iota((channels, LANES), 1)).astype(F32).astype(BF)
    lane = iota((n_dp, LANES), 1)
    picked_scale = mm(mm(pick, scales[...]).astype(BF), pad_eye)
    picked_code = mm(pick, codes[...])
    tokens_of = []
    for t in range(block):
        part = picked_code[:, (t // 2) * LANES : (t // 2 + 1) * LANES]
        if t % 2:
            part = pltpu.roll(part, channels, 1)
        part = (part * picked_scale).astype(BF).astype(F32)
        tokens_of.append(jnp.where(lane == LIVE, used, part).astype(BF))
    stacked = jnp.concatenate(tokens_of, axis=0)
    shape = (8 * n_dp, local)
    r, k = iota(shape, 0), iota(shape, 1)
    spread = jnp.logical_and(over(r, 8) == within(k, n_dp), within(r, 8) == over(k, n_dp))
    a_send[...] = mm(spread.astype(F32).astype(BF), stacked)
    a_recv[pl.ds(pl.multiple_of(d * 8, 8), 8), :] = a_send[pl.ds(pl.multiple_of(d * 8, 8), 8), :]

    pl.semaphore_wait(barrier, n_dp - 1 + Y * (n_seq - 1))

    def tile(ref, i):
        return ref.at[pl.ds(pl.multiple_of(i * 8, 8), 8), :]

    def send_a(i, carry):
        p = lax.rem(d + i, n_dp)
        remote(tile(a_send, p), tile(a_recv, d), A, p, j)
        return carry

    lax.fori_loop(1, n_dp, send_a, 0)

    def wrows(first, count):
        return wbuf.at[pl.ds(pl.multiple_of(first * rows, 16), count * rows), :]

    for b in range(HALF):
        push(
            weight.at[:, pl.ds(b * cols, cols)],
            wrows(d, 1),
            WY,
            z * Y + HALF * c + b,
            CORES * x + core,
        )

    own_mods[0] = scale[...]
    own_mods[1] = shift[...]

    @pl.when(own)
    def _():
        for py in range(Y):

            @pl.when(py == y)
            def _():
                pltpu.make_async_copy(own_mods, mods.at[slot], recv.at[MOD]).start()

            @pl.when(py != y)
            def _():
                pltpu.make_async_remote_copy(
                    src_ref=own_mods,
                    dst_ref=mods.at[slot],
                    send_sem=mod_send.at[py],
                    recv_sem=recv.at[MOD],
                    device_id=(z * Y + py, j),
                    device_id_type=MESH,
                ).start()

    def lanes(i, count):
        return pl.ds(pl.multiple_of(i * count, LANES), count)

    def send_heads(i, carry):
        h = lax.rem(head + i, heads)
        dp, seq = z * Y + lax.rem(h, Y), CORES * lax.div(h, Y) + core
        push(
            text.at[:, lanes(h, cols)],
            qkv.at[slot, pl.ds(pl.multiple_of(j * tloc, 16), tloc), :],
            TXT,
            dp,
            seq,
        )
        push(
            grad_txt.at[:, lanes(h, HD)],
            dout.at[slot, pl.ds(pl.multiple_of(j * tloc, 16), tloc), :],
            DTXT,
            dp,
            seq,
        )
        push(
            grad_img.at[:, lanes(h, HD)],
            dout.at[slot, pl.ds(pl.multiple_of(texts + j * local, 16), local), :],
            DIMG,
            dp,
            seq,
        )
        return carry

    embed_f = embed[...].astype(F32)
    embed_centred = embed_f - jnp.sum(embed_f, axis=1, keepdims=True) * (1.0 / width)

    def shard(pz):
        return (pz * Y + c * HALF) * rows

    def wshard(pz, first=0, count=HALF * rows):
        return wbuf.at[pl.ds(pl.multiple_of(shard(pz) + first, 16), count), :]

    def hop(src_z, to, sems, step, first=0, count=HALF * rows):
        ref = wshard(src_z, first, count)
        pltpu.make_async_remote_copy(
            src_ref=ref,
            dst_ref=ref,
            send_sem=ring_send,
            recv_sem=sems.at[step],
            device_id=(to * Y + y, j),
            device_id_type=MESH,
        ).start()

    def landed(src_z, sems, step, first=0, count=HALF * rows):
        ref = wshard(src_z, first, count)
        pltpu.make_async_copy(ref, ref, sems.at[step]).wait()

    other = CORES * x + (1 - c)

    def to_sibling(src_z):
        ref = wshard(src_z)
        remote(ref, ref, SIB, d, other)

    up, down = lax.rem(z + 1, n_z), lax.rem(z + n_z - 1, n_z)
    last = n_z // 2 - 1
    piece = HALF * rows // 2
    arrived(wshard(z), WY)
    hop(z, up, ring_right, 0)
    hop(z, down, ring_left, 0)
    to_sibling(z)

    def ring_step(step):
        from_left = lax.rem(z + n_z - 1 - step, n_z)
        from_right = lax.rem(z + 1 + step, n_z)
        if step < last:
            landed(from_left, ring_right, step)
            if step + 1 < last:
                hop(from_left, up, ring_right, step + 1)
            else:
                hop(from_left, up, ring_right, step + 1, 0, piece)
            landed(from_right, ring_left, step)
            if step + 1 < last:
                hop(from_right, down, ring_left, step + 1)
            else:
                hop(from_right, down, ring_left, step + 1, piece, piece)
            to_sibling(from_left)
            to_sibling(from_right)
        else:
            landed(from_left, ring_right, step, 0, piece)
            landed(from_left, ring_left, step, piece, piece)
            to_sibling(from_left)

    lax.fori_loop(0, heads, send_heads, 0)

    arrived(a_recv.at[pl.ds(0, 8 * (n_dp - 1)), :], A)
    shape = (local, 8 * n_dp)
    r, k = iota(shape, 0), iota(shape, 1)
    gather = jnp.logical_and(over(r, block) == over(k, 8), within(r, block) == within(k, 8))
    mine = mm(gather.astype(F32).astype(BF), a_recv[...].astype(BF))
    xs = mm(mine[:, :channels].astype(BF), embed[...])
    centred = xs - jnp.sum(xs, axis=1, keepdims=True) * (1.0 / width)
    inv = lax.rsqrt(jnp.sum(centred * centred, axis=1, keepdims=True) * (1.0 / width) + EPS)
    xhat = (centred * inv).astype(BF)
    inv_high, inv_low = split(inv)
    lane = iota((local, LANES), 1)
    mine = jnp.where(lane == INV_HIGH, inv_high.astype(F32), mine)
    mine = jnp.where(lane == INV_LOW, inv_low.astype(F32), mine)
    mine = jnp.where(lane == TEXT_LEN, text_len[0].astype(F32), mine)
    own_tok[...] = mine.astype(BF)

    def send_tok(i, carry):
        h = lax.rem(head + i, heads)
        push(
            own_tok,
            tok.at[pl.ds(pl.multiple_of(slot * images + j * local, 16), local), :],
            TOK,
            z * Y + lax.rem(h, Y),
            CORES * lax.div(h, Y) + core,
        )
        return carry

    lax.fori_loop(0, heads, send_tok, 0)

    back[...] = jnp.zeros_like(back)
    back[:, :channels] = mm_nt(xhat, embed[...])

    arrived(mods, MOD)
    tail = jnp.zeros((16, width), F32)
    at = iota((16, width), 0)
    for u in range(HALF):
        high, low = split(embed_centred * (1.0 + mods[u, 0]))
        amat[u * channels : (u + 1) * channels, :] = high
        amat[(HALF + u) * channels : (HALF + u + 1) * channels, :] = low
        high, low = split(mods[u, 1])
        tail = jnp.where(at == u, high.astype(F32), tail)
        tail = jnp.where(at == HALF + u, low.astype(F32), tail)
    amat[2 * HALF * channels :, :] = tail.astype(BF)

    for step in range(last + 1):
        ring_step(step)

    arrived(wbuf.at[pl.ds(0, n_z * HALF * rows), :], SIB)
    product = mm(amat[...], wbuf[...])
    for u in range(HALF):
        mixed[u] = jnp.zeros_like(mixed[u])
        high, low = split(
            product[u * channels : (u + 1) * channels]
            + product[(HALF + u) * channels : (HALF + u + 1) * channels]
        )
        mixed[u, 0, :channels] = high
        mixed[u, 1, :channels] = low
        base = 2 * HALF * channels
        const[u] = product[base + u : base + u + 1] + product[base + HALF + u : base + HALF + u + 1]

    arrived(tok, TOK)
    arrived(qkv.at[:, pl.ds(0, texts), :], TXT)
    lane = iota((images, LANES), 1)
    tlane = iota((texts, LANES), 1)
    trow = iota((texts, LANES), 0)
    for u in range(HALF):
        tk = tok[u * images : (u + 1) * images]
        tf = tk.astype(F32)
        invs = tf[:, INV_HIGH : INV_HIGH + 1] + tf[:, INV_LOW : INV_LOW + 1]
        got = (mm(tk, mixed[u, 0]) + mm(tk, mixed[u, 1])) * invs + const[u]
        qkv[u, texts:, :] = got.astype(BF)
        length = tf[0:1, TEXT_LEN : TEXT_LEN + 1]
        kaug[u, :, :HD] = qkv[u, :, HD : 2 * HD]
        kaug[u, texts:, HD:] = jnp.where(lane == LIVE, (tf - 1.0) * 1e30, 0.0).astype(BF)
        bad = jnp.logical_and(tlane == LIVE, trow.astype(F32) >= length)
        kaug[u, :texts, HD:] = jnp.where(bad, -1e30, 0.0).astype(BF)
        vaug[u, :, :HD] = qkv[u, :, 2 * HD :]
        vaug[u, :, HD:] = jnp.ones((total, LANES), BF)
        kt[u] = qkv[u, :, HD : 2 * HD].T
        vt[u, :HD, :] = qkv[u, :, 2 * HD :].T
        vt[u, HD:, :] = jnp.ones((16, total), BF)
        pick_live = (iota((8, LANES), 1) == LIVE).astype(F32).astype(BF)
        valid_row[u, :, texts:] = mm_nt(pick_live, tk)[0:1]
        valid_row[u, :, :texts] = (iota((1, texts), 1).astype(F32) < length).astype(F32)
    arrived(dout.at[:, pl.ds(texts, images), :], DIMG)
    arrived(dout.at[:, pl.ds(0, texts), :], DTXT)
    for u in range(HALF):
        dot_t[u] = dout[u].T
    dk_acc[...] = jnp.zeros_like(dk_acc)
    dv_acc[...] = jnp.zeros_like(dv_acc)

    qb = total // 3 if total % (3 * LANES) == 0 else total
    factor = 1.0 / math.sqrt(HD)
    log2e = factor * math.log2(math.e)

    def attend(i, carry):
        first = pl.multiple_of(i * qb, LANES)
        at = pl.ds(first, qb)
        for u in range(HALF):
            query = qkv[u, at, :HD]
            ones = (iota((qb, LANES), 1) == LIVE).astype(F32).astype(BF)
            score = mm_nt(kaug[u], jnp.concatenate([query, ones], axis=1))
            top = jnp.max(score, axis=0, keepdims=True)
            expo = jnp.exp2((score - top) * log2e).astype(BF)
            got = mm(vt[u], expo)
            share = 1.0 / got[HD : HD + 1]
            valid = valid_row[u, :, at]
            out_t = (got[:HD] * (share * valid)).astype(BF)
            out_buf[u, at, :] = out_t.T
            up_t = dot_t[u, :, at].astype(F32) * valid
            delta = jnp.sum(up_t * out_t.astype(F32), axis=0, keepdims=True) * share
            scaled = (up_t * share).astype(BF)
            high, low = split(delta)
            at_row = iota((LANES, qb), 0)
            tail = jnp.where(at_row == 0, -high.astype(F32), 0.0)
            tail = jnp.where(at_row == 1, -low.astype(F32), tail).astype(BF)
            dprob = mm(vaug[u], jnp.concatenate([scaled, tail], axis=0))
            dscore = expo * dprob.astype(BF)
            dv_acc[u] += mm_nt(expo, scaled)
            dk_acc[u] += mm(dscore, query)
            dq = mm(kt[u], dscore) * factor
            dqkv[u, at, :HD] = dq.T.astype(BF)
        return carry

    lax.fori_loop(0, total // qb, attend, 0)

    for u in range(HALF):
        for s in range(n_seq):
            dp = z * Y + c * HALF + u
            push(
                out_buf.at[u, pl.ds(texts + s * local, local), :],
                out_img.at[:, lanes(head, HD)],
                OIMG,
                dp,
                s,
            )
            push(
                out_buf.at[u, pl.ds(s * tloc, tloc), :],
                out_txt.at[:, lanes(head, HD)],
                OTXT,
                dp,
                s,
            )

    gram = jnp.zeros((LANES, LANES), F32)
    seen = []
    for u in range(HALF):
        dqkv[u, :, HD : 2 * HD] = (dk_acc[u] * factor).astype(BF)
        dqkv[u, :, 2 * HD :] = dv_acc[u].astype(BF)
        grad = dqkv[u, texts:, :]
        part = mm_nt(grad, mixed[u, 0])
        for s in range(n_seq):
            slab = part[s * local : (s + 1) * local]
            packed = slab[: local // 2] + pltpu.roll(slab[local // 2 :], channels, 1)
            f_send[u * n_seq + s] = packed.astype(BF)
            push(f_send.at[u * n_seq + s], f_recv.at[head], FEAT, z * Y + c * HALF + u, s)
        tk = tok[u * images : (u + 1) * images]
        tf = tk.astype(F32)
        invs = tf[:, INV_HIGH : INV_HIGH + 1] + tf[:, INV_LOW : INV_LOW + 1]
        project = jnp.sum(tf * part, axis=1, keepdims=True) * (invs * (1.0 / width))
        scaled = tf * invs
        gram += mm_tn((scaled * (invs * project)).astype(BF), tk)
        seen.append(mm_tn(scaled.astype(BF), grad)[:channels])
    spread = mm_nt(jnp.concatenate(seen, axis=0).astype(BF), wbuf[...])
    weight_grad = spread[:channels] * (1.0 + mods[0, 0])
    for u in range(1, HALF):
        weight_grad += spread[u * channels : (u + 1) * channels] * (1.0 + mods[u, 0])
    weight_grad -= jnp.sum(weight_grad, axis=1, keepdims=True) * (1.0 / width)
    embed_f = embed[...].astype(F32)
    embed_centred = embed_f - jnp.sum(embed_f, axis=1, keepdims=True) * (1.0 / width)
    weight_grad -= mm(gram[:channels, :channels].astype(BF), embed_centred.astype(BF))
    t_send[...] = weight_grad.astype(BF)

    er, ec = channels // Y, width // n_seq

    def chunk(ref, py, pj):
        return ref.at[pl.ds(pl.multiple_of(py * er, 16), er), lanes(pj, ec)]

    me = y * n_seq + j
    plane = Y * n_seq

    def send_h1(i, carry):
        py, pj = plane_peer(i)
        remote(chunk(t_send, py, pj), h1.at[me], H1, z * Y + py, pj)
        return carry

    lax.fori_loop(1, plane, send_h1, 0)
    h1[me] = chunk(t_send, y, j)[...]

    arrived(f_recv, FEAT)
    half = local // 2
    packed = jnp.sum(f_recv[...].astype(F32), axis=0)
    lane = iota((half, LANES), 1)
    feat = jnp.concatenate(
        [
            jnp.where(lane < channels, packed, 0.0),
            jnp.where(lane < channels, pltpu.roll(packed, channels, 1), 0.0),
        ],
        axis=0,
    )
    mine = own_tok[...].astype(F32)
    inv = mine[:, INV_HIGH : INV_HIGH + 1] + mine[:, INV_LOW : INV_LOW + 1]
    project = jnp.sum(mine * feat, axis=1, keepdims=True) * (inv * (1.0 / width))
    ddeq = inv * (feat - back[...] * project)
    shape = (8 * n_dp, local)
    r, k = iota(shape, 0), iota(shape, 1)
    scatter = jnp.logical_and(over(k, block) == over(r, 8), within(k, block) == within(r, 8))
    g_send[...] = mm(scatter.astype(F32).astype(BF), ddeq.astype(BF))

    def send_g(i, carry):
        p = lax.rem(d + i, n_dp)
        remote(tile(g_send, p), tile(g_recv, d), G, p, j)
        return carry

    lax.fori_loop(1, n_dp, send_g, 0)
    tile(g_recv, d)[...] = tile(g_send, d)[...]

    arrived(h1.at[pl.ds(0, plane - 1)], H1)
    h2[z] = jnp.sum(h1[...].astype(F32), axis=0).astype(BF)

    def send_h2(i, carry):
        p = lax.rem(z + i, n_z)
        remote(h2.at[z], h2.at[z], H2, p * Y + y, j)
        return carry

    lax.fori_loop(1, n_z, send_h2, 0)

    arrived(g_recv.at[pl.ds(0, 8 * (n_dp - 1)), :], G)
    blocks = codes.shape[0]
    shape = (n_dp, 8 * n_dp)
    widen = (iota(shape, 0) == over(iota(shape, 1), 8)).astype(F32).astype(BF)
    chosen = (slot_row[...] == iota((blocks, n_dp), 0)).astype(F32).astype(BF)
    chosen = mm(chosen, widen)
    row = within(iota((blocks, 8 * n_dp), 1), 8)
    returned = g_recv[...].astype(BF)
    pad_scale = mm(scales[...], pad_eye)
    codes_of = [
        mm(jnp.where(row == t, chosen, 0.0).astype(BF), returned) * pad_scale for t in range(block)
    ]
    for t in range(0, block, 2):
        code_out[:, t // 2 * LANES : (t // 2 + 1) * LANES] = codes_of[t] + pltpu.roll(
            codes_of[t + 1], channels, 1
        )

    arrived(h2.at[pl.ds(0, n_z - 1)], H2)
    chunk(h3, y, j)[...] = jnp.sum(h2[...].astype(F32), axis=0).astype(BF)

    def send_h3(i, carry):
        py, pj = plane_peer(i)
        ref = chunk(h3, y, j)
        remote(ref, ref, H3, z * Y + py, pj)
        return carry

    lax.fori_loop(1, plane, send_h3, 0)

    left_here(a_send.at[pl.ds(0, 8 * (n_dp - 1)), :], A)
    sent(weight.at[:, pl.ds(0, (HALF - 1) * cols)], weight.at[:, pl.ds(0, HALF * cols)], WY)

    @pl.when(own)
    def _():
        for py in range(Y):

            @pl.when(py != y)
            def _():
                pltpu.make_async_copy(own_mods, own_mods, mod_send.at[py]).wait()

    few = heads - 1
    sent(text.at[:, pl.ds(0, few * cols)], text, TXT)
    sent(grad_txt.at[:, pl.ds(0, few * HD)], grad_txt, DTXT)
    sent(grad_img.at[:, pl.ds(0, few * HD)], grad_img, DIMG)
    sent(tok.at[pl.ds(0, few * local), :], tok, TOK)
    left_here(wbuf.at[pl.ds(0, n_z * HALF * rows), :], SIB)
    gone = wbuf.at[pl.ds(0, (n_z - 1) * HALF * rows), :]
    pltpu.make_async_copy(gone, gone, ring_send).wait()
    sent(out_img.at[:, pl.ds(0, few * HD)], out_img, OIMG)
    sent(out_txt.at[:, pl.ds(0, few * HD)], out_txt, OTXT)
    sent(f_send.at[pl.ds(0, few)], f_send, FEAT)
    left_here(g_send.at[pl.ds(0, 8 * (n_dp - 1)), :], G)
    left_here(h1.at[pl.ds(0, plane - 1)], H1)
    left_here(h2.at[pl.ds(0, n_z - 1)], H2)
    left_here(h1.at[pl.ds(0, plane - 1)], H3)

    arrived(h1.at[pl.ds(0, plane - 1)], H3)
    embed_out[...] = h3[...].astype(F32)
    arrived(out_img, OIMG)
    arrived(out_txt, OTXT)


def per_device(
    n_dp,
    n_seq,
    latent_codes,
    latent_scales,
    send_list,
    embed_weight,
    modulation_offset,
    mod_scale,
    qkv_weight,
    text_qkv,
    text_len,
    out_grad_img,
    out_grad_txt,
):
    codes, scales = latent_codes[0, 0], latent_scales[0, 0]
    slots = send_list[0, 0]
    channels, width = embed_weight.shape
    local, tloc = out_grad_img.shape[1], out_grad_txt.shape[1]
    images, texts = local * n_seq, tloc * n_seq
    total = images + texts
    heads = Y * n_seq // CORES
    cols = 3 * HD
    n_z = n_dp // Y
    er, ec = channels // Y, width // n_seq
    vmem, hbm = pl.BlockSpec(memory_space=pltpu.VMEM), pl.BlockSpec(memory_space=pl.ANY)
    smem = pl.BlockSpec(memory_space=pltpu.SMEM)
    block = codes.shape[1]
    scratch = [
        pltpu.VMEM((8 * n_dp, LANES), F32),
        pltpu.VMEM((8 * n_dp, LANES), F32),
        pltpu.VMEM((local, LANES), BF),
        pltpu.VMEM((2, 1, width), F32),
        pltpu.VMEM((HALF * images, LANES), BF),
        pltpu.VMEM((HALF, 2, 1, width), F32),
        pltpu.VMEM((width, cols), BF),
        pltpu.VMEM((2 * HALF * channels + 16, width), BF),
        pltpu.VMEM((HALF, 2, LANES, cols), BF),
        pltpu.VMEM((HALF, 1, cols), F32),
        pltpu.VMEM((HALF, total, cols), BF),
        pltpu.VMEM((HALF, total, HD), BF),
        pltpu.VMEM((HALF, total, 2 * HD), BF),
        pltpu.VMEM((HALF, total, 2 * HD), BF),
        pltpu.VMEM((HALF, HD, total), BF),
        pltpu.VMEM((HALF, HD + 16, total), BF),
        pltpu.VMEM((HALF, HD, total), BF),
        pltpu.VMEM((HALF, 1, total), F32),
        pltpu.VMEM((HALF, total, HD), F32),
        pltpu.VMEM((HALF, total, HD), F32),
        pltpu.VMEM((HALF, total, HD), BF),
        pltpu.VMEM((HALF, total, cols), BF),
        pltpu.VMEM((heads, local // 2, LANES), BF),
        pltpu.VMEM((heads, local // 2, LANES), BF),
        pltpu.VMEM((local, LANES), F32),
        pltpu.VMEM((8 * n_dp, LANES), F32),
        pltpu.VMEM((8 * n_dp, LANES), F32),
        pltpu.VMEM((channels, width), BF),
        pltpu.VMEM((Y * n_seq, er, ec), BF),
        pltpu.VMEM((n_z, er, ec), BF),
        pltpu.VMEM((channels, width), BF),
        pltpu.SemaphoreType.DMA((16,)),
        pltpu.SemaphoreType.DMA((16,)),
        pltpu.SemaphoreType.DMA((Y,)),
        pltpu.SemaphoreType.DMA((n_z // 2,)),
        pltpu.SemaphoreType.DMA((n_z // 2,)),
        pltpu.SemaphoreType.DMA,
    ]
    out = pl.pallas_call(
        functools.partial(kernel, n_dp, n_seq),
        out_shape=(
            jax.ShapeDtypeStruct((local, heads * HD), BF),
            jax.ShapeDtypeStruct((tloc, heads * HD), BF),
            jax.ShapeDtypeStruct((codes.shape[0], block), F32),
            jax.ShapeDtypeStruct((channels, width), F32),
        ),
        in_specs=[smem] + [vmem] * 7 + [hbm] * 4,
        out_specs=(hbm, hbm, vmem, vmem),
        scratch_shapes=scratch,
        compiler_params=pltpu.CompilerParams(
            collective_id=0, has_side_effects=True, vmem_limit_bytes=48 * 1024 * 1024
        ),
    )(
        text_len,
        codes,
        scales,
        slots[:, None],
        slots[None, :],
        embed_weight,
        modulation_offset,
        mod_scale,
        qkv_weight,
        text_qkv[0],
        out_grad_img[0],
        out_grad_txt[0],
    )
    img, txt, code, grad = out
    return img[None], txt[None], code[None, None], grad


def solution(mesh):
    return jax.shard_map(
        functools.partial(per_device, mesh.shape["dp"], mesh.shape["seq"]),
        mesh=mesh,
        in_specs=(
            P("dp", "seq", None, None),
            P("dp", "seq", None, None),
            P("dp", "seq", None),
            P(),
            P("dp", None),
            P("dp", None),
            P("dp", "seq"),
            P("dp", "seq", None),
            P("dp"),
            P("dp", "seq", None),
            P("dp", "seq", None),
        ),
        out_specs=(P("dp", "seq", None), P("dp", "seq", None), P("dp", "seq", None, None), P()),
        check_vma=False,
    )
```

```python
import functools
import math

import jax
import jax.numpy as jnp
from jax import lax
from jax.experimental import pallas as pl
from jax.experimental.pallas import tpu as pltpu
from jax.sharding import PartitionSpec as P

MESH = pl.DeviceIdType.MESH
CUT = 99
BF, F32 = jnp.bfloat16, jnp.float32
HD = 128
LANES = 128
EPS = 1e-06
Y = 4
CORES = 2
HALF = Y // CORES
LIVE, INV_HIGH, INV_LOW, TEXT_LEN = 64, 65, 66, 67


def mm(a, b):
    return jnp.dot(a, b, preferred_element_type=F32)


def mm_nt(a, b):
    return lax.dot_general(a, b, (((1,), (1,)), ((), ())), preferred_element_type=F32)


def mm_tn(a, b):
    return lax.dot_general(a, b, (((0,), (0,)), ((), ())), preferred_element_type=F32)


def iota(shape, dim):
    return lax.broadcasted_iota(jnp.int32, shape, dim)


def over(value, power):
    return lax.shift_right_logical(value, jnp.full_like(value, power.bit_length() - 1))


def within(value, power):
    return jnp.bitwise_and(value, power - 1)


def query_block(total):
    return total // 3 if total % (3 * LANES) == 0 else total


def split(value):
    high = value.astype(BF)
    return high, (value - high.astype(F32)).astype(BF)


def kernel(
    n_dp,
    n_seq,
    text_len_hbm,
    codes_hbm,
    scales_hbm,
    slots_hbm,
    embed_hbm,
    shift_hbm,
    scale_hbm,
    weight,
    text,
    grad_img,
    grad_txt,
    out_img,
    out_txt,
    code_out,
    embed_out,
    text_len,
    codes,
    scales,
    slot_row,
    embed,
    a_send,
    a_recv,
    own_tok,
    own_pack,
    tokp,
    own_mods,
    tok,
    mods,
    wbuf,
    amat,
    mixed,
    qkv,
    dout,
    kaug,
    vaug,
    kt,
    vt,
    ebuf,
    sbuf,
    mixed_t,
    wbar,
    centred_b,
    valid_row,
    dk_acc,
    dv_acc,
    out_buf,
    img_recv,
    txt_recv,
    dqkv,
    f_send,
    f_recv,
    back,
    g_send,
    g_recv,
    t_send,
    h1,
    h2,
    h3,
    load,
    store,
    send,
    recv,
    mod_send,
    ring_right,
    ring_left,
    ring_send,
):
    d, j = lax.axis_index("dp"), lax.axis_index("seq")
    z, y = lax.div(d, Y), lax.rem(d, Y)
    x, c = lax.div(j, CORES), lax.rem(j, CORES)
    slot, core = lax.rem(y, HALF), lax.div(y, HALF)
    own = core == c
    head = Y * x + y
    n_z, heads = n_dp // Y, Y * n_seq // CORES
    channels, width = embed_hbm.shape
    rows = weight.shape[0]
    local = grad_img.shape[0]
    tloc = grad_txt.shape[0]
    images, texts = local * n_seq, tloc * n_seq
    total = images + texts
    block = local // n_dp
    cols = 3 * HD

    def same(dp, seq):
        return jnp.logical_and(dp == d, seq == j)

    def remote(src, dst, k, dp, seq):
        pltpu.make_async_remote_copy(
            src_ref=src,
            dst_ref=dst,
            send_sem=send.at[k],
            recv_sem=recv.at[k],
            device_id=(dp, seq),
            device_id_type=MESH,
        ).start()

    def push(src, dst, k, dp, seq):
        @pl.when(same(dp, seq))
        def _():
            pltpu.make_async_copy(src, dst, recv.at[k]).start()

        @pl.when(jnp.logical_not(same(dp, seq)))
        def _():
            remote(src, dst, k, dp, seq)

    def arrived(ref, k):
        pltpu.make_async_copy(ref, ref, recv.at[k]).wait()

    def left_here(ref, k):
        pltpu.make_async_copy(ref, ref, send.at[k]).wait()

    def sent(some, whole, k):
        @pl.when(own)
        def _():
            left_here(some, k)

        @pl.when(jnp.logical_not(own))
        def _():
            left_here(whole, k)

    A, MOD, TXT, DIMG, TOK, SIB, OIMG, OTXT, FEAT, G, H1, H2, H3, DTXT, WY = range(15)

    def plane_peer(i):
        py = lax.rem(y + lax.div(i, n_seq), Y)
        return py, lax.rem(j + lax.rem(i, n_seq), n_seq)

    loads = [
        pltpu.make_async_copy(src, dst, load.at[i])
        for i, (src, dst) in enumerate(
            (
                (slots_hbm, slot_row),
                (codes_hbm, codes),
                (scales_hbm, scales),
                (embed_hbm, embed),
                (scale_hbm, own_mods.at[0]),
                (shift_hbm, own_mods.at[1]),
                (text_len_hbm, text_len),
            )
        )
    ]
    for copy in loads:
        copy.start()

    barrier = pltpu.get_barrier_semaphore()

    def greet_dp(i, carry):
        pl.semaphore_signal(
            barrier, inc=1, device_id=(lax.rem(d + i, n_dp), j), device_id_type=MESH
        )
        return carry

    lax.fori_loop(1, n_dp, greet_dp, 0)

    def greet_plane(i, carry):
        py = lax.rem(y + lax.div(i, n_seq - 1), Y)
        pj = lax.rem(j + 1 + lax.rem(i, n_seq - 1), n_seq)
        pl.semaphore_signal(barrier, inc=1, device_id=(z * Y + py, pj), device_id_type=MESH)
        return carry

    lax.fori_loop(0, Y * (n_seq - 1), greet_plane, 0)

    for copy in loads[:3]:
        copy.wait()
    square = (n_dp, n_dp)
    diagonal = iota(square, 0) == iota(square, 1)
    slot_col = jnp.sum(
        jnp.where(diagonal, slot_row[...].astype(F32), 0.0), axis=1, keepdims=True
    ).astype(jnp.int32)
    pick = (slot_col == iota((n_dp, codes.shape[0]), 1)).astype(F32).astype(BF)
    used = jnp.sum(pick.astype(F32), axis=1, keepdims=True)
    pad_eye = (iota((channels, LANES), 0) == iota((channels, LANES), 1)).astype(F32).astype(BF)
    lane = iota((n_dp, LANES), 1)
    picked_scale = mm(mm(pick, scales[...]).astype(BF), pad_eye)
    picked_code = mm(pick, codes[...])
    for t in range(block):
        part = picked_code[:, (t // 2) * LANES : (t // 2 + 1) * LANES]
        if t % 2:
            part = pltpu.roll(part, channels, 1)
        part = (part * picked_scale).astype(BF).astype(F32)
        a_send[:, t, :] = jnp.where(lane == LIVE, used, part)
    a_recv[d] = a_send[d]

    pl.semaphore_wait(barrier, n_dp - 1 + Y * (n_seq - 1))

    def wrows(first, count):
        return wbuf.at[pl.ds(pl.multiple_of(first * rows, 16), count * rows), :]

    for b in range(HALF):
        push(
            weight.at[:, pl.ds(b * cols, cols)],
            wrows(d, 1),
            WY + slot,
            z * Y + HALF * c + b,
            CORES * x + core,
        )

    def send_a(i, carry):
        p = lax.rem(d + i, n_dp)
        remote(a_send.at[p], a_recv.at[d], A, p, j)
        return carry

    lax.fori_loop(1, n_dp, send_a, 0)

    for copy in loads[3:]:
        copy.wait()

    @pl.when(own)
    def _():
        for py in range(Y):

            @pl.when(py == y)
            def _():
                pltpu.make_async_copy(own_mods, mods.at[slot], recv.at[MOD]).start()

            @pl.when(py != y)
            def _():
                pltpu.make_async_remote_copy(
                    src_ref=own_mods,
                    dst_ref=mods.at[slot],
                    send_sem=mod_send.at[py],
                    recv_sem=recv.at[MOD],
                    device_id=(z * Y + py, j),
                    device_id_type=MESH,
                ).start()

    def lanes(i, count):
        return pl.ds(pl.multiple_of(i * count, LANES), count)

    def chip_of(i):
        h = lax.rem(head + i, heads)
        return h, z * Y + lax.rem(h, Y), CORES * lax.div(h, Y) + core

    def send_text(i, carry):
        h, dp, seq = chip_of(i)
        here = pl.ds(pl.multiple_of(j * tloc, 16), tloc)
        push(text.at[:, lanes(h, cols)], qkv.at[slot, here, :], TXT, dp, seq)
        return carry

    def send_grad(i, carry):
        h, dp, seq = chip_of(i)
        here = pl.ds(pl.multiple_of(j * tloc, 16), tloc)
        push(grad_txt.at[:, lanes(h, HD)], dout.at[slot, here, :], DTXT, dp, seq)
        here = pl.ds(pl.multiple_of(texts + j * local, 16), local)
        push(grad_img.at[:, lanes(h, HD)], dout.at[slot, here, :], DIMG, dp, seq)
        return carry

    embed_f = embed[...].astype(F32)
    embed_centred = embed_f - jnp.sum(embed_f, axis=1, keepdims=True) * (1.0 / width)

    def piece(pz, p):
        return wrows(pz * Y + c * HALF + p, 1)

    def hop(pz, p, to, sems, step):
        pltpu.make_async_remote_copy(
            src_ref=piece(pz, p),
            dst_ref=piece(pz, p),
            send_sem=ring_send,
            recv_sem=sems.at[step, p],
            device_id=(to * Y + y, j),
            device_id_type=MESH,
        ).start()

    def landed(pz, p, sems, step):
        pltpu.make_async_copy(piece(pz, p), piece(pz, p), sems.at[step, p]).wait()

    def to_sibling(pz, p):
        remote(piece(pz, p), piece(pz, p), SIB, d, CORES * x + (1 - c))

    up, down = lax.rem(z + 1, n_z), lax.rem(z + n_z - 1, n_z)
    last = n_z // 2 - 1
    for p in range(HALF):
        arrived(piece(z, p), WY + p)
        hop(z, p, up, ring_right, 0)
        hop(z, p, down, ring_left, 0)
        to_sibling(z, p)

    def ring_step(step):
        from_left = lax.rem(z + n_z - 1 - step, n_z)
        from_right = lax.rem(z + 1 + step, n_z)
        for p in range(HALF):
            if step < last:
                landed(from_left, p, ring_right, step)
                if step + 1 < last or p == 0:
                    hop(from_left, p, up, ring_right, step + 1)
                landed(from_right, p, ring_left, step)
                if step + 1 < last or p == 1:
                    hop(from_right, p, down, ring_left, step + 1)
                to_sibling(from_left, p)
                to_sibling(from_right, p)
            else:
                landed(from_left, p, (ring_right, ring_left)[p], step)
                to_sibling(from_left, p)

    lax.fori_loop(0, heads, send_text, 0)

    arrived(a_recv.at[pl.ds(0, n_dp - 1)], A)
    shape = (local, local)
    r, k = iota(shape, 0), iota(shape, 1)
    gather = jnp.logical_and(over(r, block) == within(k, n_dp), within(r, block) == over(k, n_dp))
    gather = gather.astype(F32).astype(BF)
    stacked = jnp.concatenate([a_recv[:, t, :] for t in range(block)], axis=0)
    mine = mm(gather, stacked.astype(BF))
    xs = mm(mine[:, :channels].astype(BF), embed[...])
    centred = xs - jnp.sum(xs, axis=1, keepdims=True) * (1.0 / width)
    inv = lax.rsqrt(jnp.sum(centred * centred, axis=1, keepdims=True) * (1.0 / width) + EPS)
    xhat = (centred * inv).astype(BF)
    inv_high, inv_low = split(inv)
    lane = iota((local, LANES), 1)
    mine = jnp.where(lane == INV_HIGH, inv_high.astype(F32), mine)
    mine = jnp.where(lane == INV_LOW, inv_low.astype(F32), mine)
    mine = jnp.where(lane == TEXT_LEN, text_len[0].astype(F32), mine)
    own_tok[...] = mine.astype(BF)
    half = local // 2
    only = jnp.where(lane < channels, mine, 0.0)
    own_pack[:half] = (only[:half] + pltpu.roll(only[half:], channels, 1)).astype(BF)
    flag = (iota((16, LANES), 1) == iota((16, LANES), 0) + LIVE).astype(F32).astype(BF)
    own_pack[half:] = jnp.zeros((16, LANES), BF)
    own_pack[half:, :local] = mm_nt(flag, own_tok[...]).astype(BF)

    def send_tok(i, carry):
        h, dp, seq = chip_of(i)
        push(own_pack, tokp.at[slot * n_seq + j], TOK, dp, seq)
        return carry

    lax.fori_loop(0, heads, send_tok, 0)
    ring_step(0)
    back[...] = jnp.zeros_like(back)
    back[:, :channels] = mm_nt(xhat, embed[...])

    arrived(mods, MOD)
    tail = jnp.zeros((16, width), F32)
    at = iota((16, width), 0)
    for u in range(HALF):
        high, low = split(embed_centred * (1.0 + mods[u, 0]))
        amat[u * channels : (u + 1) * channels, :] = high
        amat[(HALF + u) * channels : (HALF + u + 1) * channels, :] = low
        high, low = split(mods[u, 1])
        tail = jnp.where(at == u, high.astype(F32), tail)
        tail = jnp.where(at == HALF + u, low.astype(F32), tail)
        high, low = split((1.0 + mods[u, 0]) * (1.0 / width))
        tail = jnp.where(at == 2 * HALF + u, high.astype(F32), tail)
        tail = jnp.where(at == 3 * HALF + u, low.astype(F32), tail)
    amat[2 * HALF * channels :, :] = tail.astype(BF)
    centred_b[...] = embed_centred.astype(BF)

    for step in range(1, last):
        ring_step(step)

    arrived(tokp, TOK)
    half = local // 2
    low_lane = iota((half, LANES), 1) < channels
    for i in range(heads):
        packed = tokp[i, :half].astype(F32)
        flags = mm_tn(tokp[i, half:], flag)
        first = jnp.where(low_lane, packed, 0.0) + flags[:half]
        second = jnp.where(low_lane, pltpu.roll(packed, channels, 1), 0.0) + flags[half:local]
        tok[i * local : i * local + half] = first.astype(BF)
        tok[i * local + half : (i + 1) * local] = second.astype(BF)

    lane = iota((images, LANES), 1)
    tlane = iota((texts, LANES), 1)
    trow = iota((texts, LANES), 0)
    inv_rows = []
    for u in range(HALF):
        tk = tok[u * images : (u + 1) * images]
        tf = tk.astype(F32)
        length = tf[0:1, TEXT_LEN : TEXT_LEN + 1]
        kaug[u, texts:, HD:] = jnp.where(lane == LIVE, (tf - 1.0) * 1e30, 0.0).astype(BF)
        bad = jnp.logical_and(tlane == LIVE, trow.astype(F32) >= length)
        kaug[u, :texts, HD:] = jnp.where(bad, -1e30, 0.0).astype(BF)
        vaug[u, :, HD:] = jnp.ones((total, LANES), BF)
        vt[u, HD:, :] = jnp.ones((16, total), BF)
        flag_rows = mm_nt(flag, tk)
        inv_rows.append(flag_rows[1:2] + flag_rows[2:3])
        valid_row[u, :, texts:] = flag_rows[0:1]
        valid_row[u, :, :texts] = (iota((1, texts), 1).astype(F32) < length).astype(F32)
    dk_acc[...] = jnp.zeros_like(dk_acc)
    dv_acc[...] = jnp.zeros_like(dv_acc)
    arrived(qkv.at[:, pl.ds(0, texts), :], TXT)
    for u in range(HALF):
        kaug[u, :texts, :HD] = qkv[u, :texts, HD : 2 * HD]
        vaug[u, :texts, :HD] = qkv[u, :texts, 2 * HD :]
        kt[u, :, :texts] = qkv[u, :texts, HD : 2 * HD].T
        vt[u, :HD, :texts] = qkv[u, :texts, 2 * HD :].T

    lax.fori_loop(0, heads, send_grad, 0)
    ring_step(last)
    arrived(wbuf.at[pl.ds(0, n_z * HALF * rows), :], SIB)
    product = mm(amat[...], wbuf[...])
    base = 2 * HALF * channels
    for u in range(HALF):
        sums = (
            product[u * channels : (u + 1) * channels]
            + product[(HALF + u) * channels : (HALF + u + 1) * channels]
        )
        sums = jnp.concatenate([sums, jnp.zeros((LANES - channels, cols), F32)], axis=0)
        mixed[u, 0], mixed[u, 1] = split(sums)
        mixed_t[u, 0], mixed_t[u, 1] = split(sums.T)
        const = product[base + u : base + u + 1] + product[base + HALF + u : base + HALF + u + 1]
        wbar[u] = (
            product[base + 2 * HALF + u : base + 2 * HALF + u + 1]
            + product[base + 3 * HALF + u : base + 3 * HALF + u + 1]
        )
        const_t = jnp.broadcast_to(const[:, HD:], (LANES, 2 * HD)).T
        tk = tok[u * images : (u + 1) * images]
        tf = tk.astype(F32)
        invs = tf[:, INV_HIGH : INV_HIGH + 1] + tf[:, INV_LOW : INV_LOW + 1]
        got = ((mm(tk, mixed[u, 0]) + mm(tk, mixed[u, 1])) * invs + const).astype(BF)
        qkv[u, texts:, :HD] = got[:, :HD]
        kaug[u, texts:, :HD] = got[:, HD : 2 * HD]
        vaug[u, texts:, :HD] = got[:, 2 * HD :]
        got = mm_nt(mixed_t[u, 0, HD:], tk) + mm_nt(mixed_t[u, 1, HD:], tk)
        got = (got * inv_rows[u] + const_t[:, 0:1]).astype(BF)
        kt[u, :, texts:] = got[:HD]
        vt[u, :HD, texts:] = got[HD:]

    qb = query_block(total)
    factor = 1.0 / math.sqrt(HD)
    log2e = factor * math.log2(math.e)

    def attend(i, carry):
        first = pl.multiple_of(i * qb, LANES)
        at = pl.ds(first, qb)
        for u in range(HALF):
            query = qkv[u, at, :HD]
            ones = (iota((qb, LANES), 1) == LIVE).astype(F32).astype(BF)
            score = mm_nt(kaug[u], jnp.concatenate([query, ones], axis=1))
            top = jnp.max(score, axis=0, keepdims=True)
            expo = jnp.exp2((score - top) * log2e).astype(BF)
            got = mm(vt[u], expo)
            share = valid_row[u, :, at] / got[HD : HD + 1]
            out_buf[u, at, :] = (got[:HD] * share).T.astype(BF)
            sbuf[u, at, :] = jnp.broadcast_to(share, (LANES, qb)).T
            ebuf[u, i] = expo
        for u in range(HALF):
            dp = z * Y + c * HALF + u
            for s in range(n_seq):

                @pl.when(i == (texts + s * local) // qb)
                def _():
                    push(
                        out_buf.at[u, pl.ds(texts + s * local, local), :],
                        img_recv.at[:, lanes(head, HD)],
                        OIMG,
                        dp,
                        s,
                    )

                @pl.when(i == 0)
                def _():
                    push(
                        out_buf.at[u, pl.ds(s * tloc, tloc), :],
                        txt_recv.at[:, lanes(head, HD)],
                        OTXT,
                        dp,
                        s,
                    )

        return carry

    lax.fori_loop(0, total // qb, attend, 0)

    def attend_back(i, carry):
        at = pl.ds(pl.multiple_of(i * qb, LANES), qb)
        lane = iota((qb, LANES), 1)
        for u in range(HALF):
            expo = ebuf[u, i]
            share = sbuf[u, at, :]
            up = dout[u, at, :].astype(F32)
            delta = jnp.sum(up * out_buf[u, at, :].astype(F32), axis=1, keepdims=True) * share
            scaled = (up * share).astype(BF)
            high, low = split(delta)
            tail = jnp.where(lane == 0, -high.astype(F32), 0.0)
            tail = jnp.where(lane == 1, -low.astype(F32), tail).astype(BF)
            dprob = mm_nt(vaug[u], jnp.concatenate([scaled, tail], axis=1))
            dscore = expo * dprob.astype(BF)
            dv_acc[u] += mm(expo, scaled)
            dk_acc[u] += mm(dscore, qkv[u, at, :HD])
            dqkv[u, at, :HD] = (mm(kt[u], dscore) * factor).T.astype(BF)
        return carry

    arrived(dout.at[:, pl.ds(texts, images), :], DIMG)
    arrived(dout.at[:, pl.ds(0, texts), :], DTXT)
    lax.fori_loop(0, total // qb, attend_back, 0)

    gram = jnp.zeros((LANES, LANES), F32)
    seen = []
    for u in range(HALF):
        dqkv[u, :, HD : 2 * HD] = (dk_acc[u] * factor).astype(BF)
        dqkv[u, :, 2 * HD :] = dv_acc[u].astype(BF)
        grad = dqkv[u, texts:, :]
        part = mm(grad, mixed_t[u, 0])
        for s in range(n_seq):
            slab = part[s * local : (s + 1) * local]
            packed = slab[: local // 2] + pltpu.roll(slab[local // 2 :], channels, 1)
            f_send[u * n_seq + s] = packed.astype(BF)
            push(f_send.at[u * n_seq + s], f_recv.at[head], FEAT, z * Y + c * HALF + u, s)
        tk = tok[u * images : (u + 1) * images]
        tf = tk.astype(F32)
        invs = tf[:, INV_HIGH : INV_HIGH + 1] + tf[:, INV_LOW : INV_LOW + 1]
        project = jnp.sum(tf * part, axis=1, keepdims=True) * (invs * (1.0 / width))
        scaled = tf * invs
        gram += mm_tn((scaled * (invs * project)).astype(BF), tk)
        seen.append(mm_tn(scaled.astype(BF), grad)[:channels])
    seen = jnp.concatenate(seen, axis=0).astype(BF)
    gram = gram[:channels, :channels].astype(BF)
    average = jnp.zeros((channels, 1), F32)
    for u in range(HALF):
        mine = seen[u * channels : (u + 1) * channels].astype(F32)
        average += jnp.sum(mine * wbar[u], axis=1, keepdims=True)

    er, ec = channels // Y, width // n_seq

    def chunk(ref, py, pj):
        return ref.at[pl.ds(pl.multiple_of(py * er, 16), er), lanes(pj, ec)]

    me = y * n_seq + j
    plane = Y * n_seq

    def weight_block(i, carry):
        q = lax.rem(j + i, n_seq)
        at = lanes(q, ec)
        spread = mm_nt(seen, wbuf[pl.ds(pl.multiple_of(q * ec, LANES), ec), :])
        part = -mm(gram, centred_b[:, at]) - average
        for u in range(HALF):
            part += spread[u * channels : (u + 1) * channels] * (1.0 + mods[u, 0, :, at])
        t_send[:, at] = part.astype(BF)
        for py in range(Y):

            @pl.when(jnp.logical_not(jnp.logical_and(py == y, q == j)))
            def _():
                remote(chunk(t_send, py, q), h1.at[me], H1, z * Y + py, q)

        return carry

    lax.fori_loop(0, n_seq, weight_block, 0)
    h1[me] = chunk(t_send, y, j)[...]

    arrived(f_recv, FEAT)
    half = local // 2
    packed = jnp.sum(f_recv[...].astype(F32), axis=0)
    lane = iota((half, LANES), 1)
    feat = jnp.concatenate(
        [
            jnp.where(lane < channels, packed, 0.0),
            jnp.where(lane < channels, pltpu.roll(packed, channels, 1), 0.0),
        ],
        axis=0,
    )
    mine = own_tok[...].astype(F32)
    inv = mine[:, INV_HIGH : INV_HIGH + 1] + mine[:, INV_LOW : INV_LOW + 1]
    project = jnp.sum(mine * feat, axis=1, keepdims=True) * (inv * (1.0 / width))
    ddeq = inv * (feat - back[...] * project)
    spread = mm_tn(gather, ddeq.astype(BF))
    for t in range(block):
        g_send[:, t, :] = spread[t * n_dp : (t + 1) * n_dp]

    def send_g(i, carry):
        p = lax.rem(d + i, n_dp)
        remote(g_send.at[p], g_recv.at[d], G, p, j)
        return carry

    lax.fori_loop(1, n_dp, send_g, 0)
    g_recv[d] = g_send[d]

    arrived(h1.at[pl.ds(0, plane - 1)], H1)
    h2[z] = jnp.sum(h1[...].astype(F32), axis=0).astype(BF)

    def send_h2(i, carry):
        p = lax.rem(z + i, n_z)
        remote(h2.at[z], h2.at[z], H2, p * Y + y, j)
        return carry

    lax.fori_loop(1, n_z, send_h2, 0)

    arrived(h2.at[pl.ds(0, n_z - 1)], H2)
    chunk(h3, y, j)[...] = jnp.sum(h2[...].astype(F32), axis=0).astype(BF)

    def send_h3(i, carry):
        py, pj = plane_peer(i)
        ref = chunk(h3, y, j)
        remote(ref, ref, H3, z * Y + py, pj)
        return carry

    lax.fori_loop(1, plane, send_h3, 0)

    arrived(img_recv, OIMG)
    arrived(txt_recv, OTXT)
    stores = [
        pltpu.make_async_copy(img_recv, out_img, store.at[0]),
        pltpu.make_async_copy(txt_recv, out_txt, store.at[1]),
    ]
    for copy in stores:
        copy.start()

    arrived(g_recv.at[pl.ds(0, n_dp - 1)], G)
    blocks = codes.shape[0]
    chosen = (slot_row[...] == iota((blocks, n_dp), 0)).astype(F32).astype(BF)
    pad_scale = mm(scales[...], pad_eye)
    codes_of = [mm(chosen, g_recv[:, t, :].astype(BF)) * pad_scale for t in range(block)]
    for t in range(0, block, 2):
        code_out[:, 0, t // 2 * LANES : (t // 2 + 1) * LANES] = codes_of[t] + pltpu.roll(
            codes_of[t + 1], channels, 1
        )

    left_here(a_send.at[pl.ds(0, n_dp - 1)], A)
    sent(weight.at[:, pl.ds(0, (HALF - 1) * cols)], weight.at[:, pl.ds(0, HALF * cols)], WY + slot)

    @pl.when(own)
    def _():
        for py in range(Y):

            @pl.when(py != y)
            def _():
                pltpu.make_async_copy(own_mods, own_mods, mod_send.at[py]).wait()

    few = heads - 1
    sent(text.at[:, pl.ds(0, few * cols)], text, TXT)
    sent(grad_txt.at[:, pl.ds(0, few * HD)], grad_txt, DTXT)
    sent(grad_img.at[:, pl.ds(0, few * HD)], grad_img, DIMG)
    sent(tokp.at[pl.ds(0, few)], tokp, TOK)
    left_here(wbuf.at[pl.ds(0, n_z * HALF * rows), :], SIB)
    gone = wbuf.at[pl.ds(0, (n_z - 1) * HALF * rows), :]
    pltpu.make_async_copy(gone, gone, ring_send).wait()
    sent(img_recv.at[:, pl.ds(0, few * HD)], img_recv, OIMG)
    sent(txt_recv.at[:, pl.ds(0, few * HD)], txt_recv, OTXT)
    sent(f_send.at[pl.ds(0, few)], f_send, FEAT)
    left_here(g_send.at[pl.ds(0, n_dp - 1)], G)
    left_here(h1.at[pl.ds(0, plane - 1)], H1)
    left_here(h2.at[pl.ds(0, n_z - 1)], H2)
    left_here(h1.at[pl.ds(0, plane - 1)], H3)

    arrived(h1.at[pl.ds(0, plane - 1)], H3)
    to_hbm = pltpu.make_async_copy(h3, embed_out, store.at[2])
    to_hbm.start()
    to_hbm.wait()
    for copy in stores:
        copy.wait()


def finish(*refs):
    sources, results, held = refs[:4], refs[4:8], refs[8:12]
    wide, came, went = refs[12:]
    inward = [
        pltpu.make_async_copy(sources[i], held[i], came.at[i]) for i in (3, 0, 1, 2)
    ]
    for copy in inward:
        copy.start()
    inward[0].wait()
    wide[...] = held[3][...].astype(F32)
    last = pltpu.make_async_copy(wide, results[3], went.at[3])
    last.start()
    outward = [pltpu.make_async_copy(held[i], results[i], went.at[i]) for i in range(3)]
    for before, copy in zip(inward[1:], outward):
        before.wait()
        copy.start()
    for copy in outward:
        copy.wait()
    last.wait()


def per_device(
    n_dp,
    n_seq,
    latent_codes,
    latent_scales,
    send_list,
    embed_weight,
    modulation_offset,
    mod_scale,
    qkv_weight,
    text_qkv,
    text_len,
    out_grad_img,
    out_grad_txt,
):
    codes, scales = latent_codes[0, 0], latent_scales[0, 0]
    slots = send_list[0, 0]
    channels, width = embed_weight.shape
    local, tloc = out_grad_img.shape[1], out_grad_txt.shape[1]
    images, texts = local * n_seq, tloc * n_seq
    total = images + texts
    heads = Y * n_seq // CORES
    cols = 3 * HD
    n_z = n_dp // Y
    er, ec = channels // Y, width // n_seq
    qb = query_block(total)
    vmem, hbm = pl.BlockSpec(memory_space=pltpu.VMEM), pl.BlockSpec(memory_space=pltpu.HBM)
    block = codes.shape[1]
    scratch = [
        pltpu.SMEM((1,), jnp.int32),
        pltpu.VMEM(codes.shape, BF),
        pltpu.VMEM(scales.shape, BF),
        pltpu.VMEM((1, n_dp), jnp.int32),
        pltpu.VMEM((channels, width), BF),
        pltpu.VMEM((n_dp, 4, LANES), F32),
        pltpu.VMEM((n_dp, 4, LANES), F32),
        pltpu.VMEM((local, LANES), BF),
        pltpu.VMEM((local // 2 + 16, LANES), BF),
        pltpu.VMEM((heads, local // 2 + 16, LANES), BF),
        pltpu.VMEM((2, 1, width), F32),
        pltpu.VMEM((HALF * images, LANES), BF),
        pltpu.VMEM((HALF, 2, 1, width), F32),
        pltpu.VMEM((width, cols), BF),
        pltpu.VMEM((2 * HALF * channels + 16, width), BF),
        pltpu.VMEM((HALF, 2, LANES, cols), BF),
        pltpu.VMEM((HALF, total, cols), BF),
        pltpu.VMEM((HALF, total, HD), BF),
        pltpu.VMEM((HALF, total, 2 * HD), BF),
        pltpu.VMEM((HALF, total, 2 * HD), BF),
        pltpu.VMEM((HALF, HD, total), BF),
        pltpu.VMEM((HALF, HD + 16, total), BF),
        pltpu.VMEM((HALF, total // qb, total, qb), BF),
        pltpu.VMEM((HALF, total, LANES), F32),
        pltpu.VMEM((HALF, 2, cols, LANES), BF),
        pltpu.VMEM((HALF, 1, cols), F32),
        pltpu.VMEM((channels, width), BF),
        pltpu.VMEM((HALF, 1, total), F32),
        pltpu.VMEM((HALF, total, HD), F32),
        pltpu.VMEM((HALF, total, HD), F32),
        pltpu.VMEM((HALF, total, HD), BF),
        pltpu.VMEM((local, heads * HD), BF),
        pltpu.VMEM((tloc, heads * HD), BF),
        pltpu.VMEM((HALF, total, cols), BF),
        pltpu.VMEM((heads, local // 2, LANES), BF),
        pltpu.VMEM((heads, local // 2, LANES), BF),
        pltpu.VMEM((local, LANES), F32),
        pltpu.VMEM((n_dp, 4, LANES), F32),
        pltpu.VMEM((n_dp, 4, LANES), F32),
        pltpu.VMEM((channels, width), BF),
        pltpu.VMEM((Y * n_seq, er, ec), BF),
        pltpu.VMEM((n_z, er, ec), BF),
        pltpu.VMEM((channels, width), BF),
        pltpu.SemaphoreType.DMA((7,)),
        pltpu.SemaphoreType.DMA((3,)),
        pltpu.SemaphoreType.DMA((16,)),
        pltpu.SemaphoreType.DMA((16,)),
        pltpu.SemaphoreType.DMA((Y,)),
        pltpu.SemaphoreType.DMA((n_z // 2, HALF)),
        pltpu.SemaphoreType.DMA((n_z // 2, HALF)),
        pltpu.SemaphoreType.DMA,
    ]
    out = pl.pallas_call(
        functools.partial(kernel, n_dp, n_seq),
        out_shape=(
            jax.ShapeDtypeStruct((local, heads * HD), BF),
            jax.ShapeDtypeStruct((tloc, heads * HD), BF),
            jax.ShapeDtypeStruct((codes.shape[0], 1, block), F32),
            jax.ShapeDtypeStruct((channels, width), BF),
        ),
        in_specs=[hbm] * 11,
        out_specs=(hbm, hbm, vmem, hbm),
        scratch_shapes=scratch,
        compiler_params=pltpu.CompilerParams(
            collective_id=0, has_side_effects=True, vmem_limit_bytes=61 * 1024 * 1024
        ),
    )(
        text_len,
        codes,
        scales,
        slots[None, :],
        embed_weight,
        modulation_offset,
        mod_scale,
        qkv_weight,
        text_qkv[0],
        out_grad_img[0],
        out_grad_txt[0],
    )
    img, txt, code, grad = pl.pallas_call(
        finish,
        out_shape=tuple(
            jax.ShapeDtypeStruct(part.shape, kind) for part, kind in zip(out, (BF, BF, F32, F32))
        ),
        in_specs=[hbm] * 4,
        out_specs=(hbm,) * 4,
        scratch_shapes=[pltpu.VMEM(part.shape, part.dtype) for part in out]
        + [
            pltpu.VMEM((channels, width), F32),
            pltpu.SemaphoreType.DMA((4,)),
            pltpu.SemaphoreType.DMA((4,)),
        ],
        compiler_params=pltpu.CompilerParams(vmem_limit_bytes=61 * 1024 * 1024),
    )(*out)
    return img[None], txt[None], code[:, 0][None, None], grad


def solution(mesh):
    return jax.shard_map(
        functools.partial(per_device, mesh.shape["dp"], mesh.shape["seq"]),
        mesh=mesh,
        in_specs=(
            P("dp", "seq", None, None),
            P("dp", "seq", None, None),
            P("dp", "seq", None),
            P(),
            P("dp", None),
            P("dp", None),
            P("dp", "seq"),
            P("dp", "seq", None),
            P("dp"),
            P("dp", "seq", None),
            P("dp", "seq", None),
        ),
        out_specs=(P("dp", "seq", None), P("dp", "seq", None), P("dp", "seq", None, None), P()),
        check_vma=False,
    )
```

```python
import functools
import math

import jax
import jax.numpy as jnp
from jax import lax
from jax.experimental import pallas as pl
from jax.experimental.pallas import tpu as pltpu
from jax.sharding import PartitionSpec as P

MESH = pl.DeviceIdType.MESH
CUT = 99
BF, F32 = jnp.bfloat16, jnp.float32
HD = 128
LANES = 128
EPS = 1e-06
Y = 4
CORES = 2
HALF = Y // CORES
LIVE, INV_HIGH, INV_LOW, TEXT_LEN = 64, 65, 66, 67


def mm(a, b):
    return jnp.dot(a, b, preferred_element_type=F32)


def mm_nt(a, b):
    return lax.dot_general(a, b, (((1,), (1,)), ((), ())), preferred_element_type=F32)


def mm_tn(a, b):
    return lax.dot_general(a, b, (((0,), (0,)), ((), ())), preferred_element_type=F32)


def iota(shape, dim):
    return lax.broadcasted_iota(jnp.int32, shape, dim)


def over(value, power):
    return lax.shift_right_logical(value, jnp.full_like(value, power.bit_length() - 1))


def within(value, power):
    return jnp.bitwise_and(value, power - 1)


def split(value):
    high = value.astype(BF)
    return high, (value - high.astype(F32)).astype(BF)


def kernel(
    n_dp,
    n_seq,
    text_len_hbm,
    codes_hbm,
    scales_hbm,
    slots_hbm,
    embed_hbm,
    shift_hbm,
    scale_hbm,
    weight,
    text,
    grad_img,
    grad_txt,
    out_img,
    out_txt,
    code_out,
    embed_out,
    text_len,
    codes,
    scales,
    slot_row,
    embed,
    a_send,
    a_recv,
    own_tok,
    own_pack,
    tokp,
    own_mods,
    tok,
    mods,
    wbuf,
    amat,
    mixed,
    qkv,
    dout,
    kaug,
    vaug,
    kt,
    vt,
    ebuf,
    sbuf,
    mixed_t,
    wbar,
    centred_b,
    inv_row,
    scaled_t,
    valid_row,
    out_buf,
    img_recv,
    txt_recv,
    dqkv,
    f_send,
    f_recv,
    back,
    g_send,
    g_recv,
    t_send,
    h1,
    h2,
    h3,
    whole,
    load,
    store,
    send,
    recv,
    mod_send,
    ring_right,
    ring_left,
    ring_send,
):
    d, j = lax.axis_index("dp"), lax.axis_index("seq")
    z, y = lax.div(d, Y), lax.rem(d, Y)
    x, c = lax.div(j, CORES), lax.rem(j, CORES)
    slot, core = lax.rem(y, HALF), lax.div(y, HALF)
    own = core == c
    head = Y * x + y
    n_z, heads = n_dp // Y, Y * n_seq // CORES
    channels, width = embed_hbm.shape
    rows = weight.shape[0]
    local = grad_img.shape[0]
    tloc = grad_txt.shape[0]
    images, texts = local * n_seq, tloc * n_seq
    total = images + texts
    block = local // n_dp
    cols = 3 * HD

    def same(dp, seq):
        return jnp.logical_and(dp == d, seq == j)

    def remote(src, dst, k, dp, seq):
        pltpu.make_async_remote_copy(
            src_ref=src,
            dst_ref=dst,
            send_sem=send.at[k],
            recv_sem=recv.at[k],
            device_id=(dp, seq),
            device_id_type=MESH,
        ).start()

    def push(src, dst, k, dp, seq):
        @pl.when(same(dp, seq))
        def _():
            pltpu.make_async_copy(src, dst, recv.at[k]).start()

        @pl.when(jnp.logical_not(same(dp, seq)))
        def _():
            remote(src, dst, k, dp, seq)

    def each(send_one):
        send_one(0, push)

        def others(i, carry):
            send_one(i, remote)
            return carry

        lax.fori_loop(1, heads, others, 0)

    def arrived(ref, k):
        pltpu.make_async_copy(ref, ref, recv.at[k]).wait()

    def left_here(ref, k):
        pltpu.make_async_copy(ref, ref, send.at[k]).wait()

    def sent(some, whole, k):
        @pl.when(own)
        def _():
            left_here(some, k)

        @pl.when(jnp.logical_not(own))
        def _():
            left_here(whole, k)

    A, MOD, TXT, DIMG, TOK, SIB, OIMG, OTXT, FEAT, G, H1, H2, H3, DTXT, WY = range(15)

    def plane_peer(i):
        py = lax.rem(y + lax.div(i, n_seq) + Y // 2, Y)
        return py, lax.rem(j + lax.rem(i, n_seq), n_seq)

    loads = [
        pltpu.make_async_copy(src, dst, load.at[i])
        for i, (src, dst) in enumerate(
            (
                (slots_hbm, slot_row),
                (codes_hbm, codes),
                (scales_hbm, scales),
                (embed_hbm, embed),
                (scale_hbm, own_mods.at[0]),
                (shift_hbm, own_mods.at[1]),
                (text_len_hbm, text_len),
            )
        )
    ]
    for copy in loads:
        copy.start()

    barrier = pltpu.get_barrier_semaphore()

    def greet_dp(i, carry):
        pl.semaphore_signal(
            barrier, inc=1, device_id=(lax.rem(d + i, n_dp), j), device_id_type=MESH
        )
        return carry

    lax.fori_loop(1, n_dp, greet_dp, 0)

    def greet_plane(i, carry):
        py = lax.rem(y + lax.div(i, n_seq - 1), Y)
        pj = lax.rem(j + 1 + lax.rem(i, n_seq - 1), n_seq)
        pl.semaphore_signal(barrier, inc=1, device_id=(z * Y + py, pj), device_id_type=MESH)
        return carry

    lax.fori_loop(0, Y * (n_seq - 1), greet_plane, 0)

    for copy in loads[:3]:
        copy.wait()
    square = (n_dp, n_dp)
    diagonal = iota(square, 0) == iota(square, 1)
    slot_col = jnp.sum(
        jnp.where(diagonal, slot_row[...].astype(F32), 0.0), axis=1, keepdims=True
    ).astype(jnp.int32)
    pick = (slot_col == iota((n_dp, codes.shape[0]), 1)).astype(F32).astype(BF)
    used = jnp.sum(pick.astype(F32), axis=1, keepdims=True)
    pad_eye = (iota((channels, LANES), 0) == iota((channels, LANES), 1)).astype(F32).astype(BF)
    lane = iota((n_dp, LANES), 1)
    picked_scale = mm(mm(pick, scales[...]).astype(BF), pad_eye)
    picked_code = mm(pick, codes[...])
    for t in range(block):
        part = picked_code[:, (t // 2) * LANES : (t // 2 + 1) * LANES]
        if t % 2:
            part = pltpu.roll(part, channels, 1)
        part = (part * picked_scale).astype(BF).astype(F32)
        a_send[:, t, :] = jnp.where(lane == LIVE, used, part)
    a_recv[d] = a_send[d]

    pl.semaphore_wait(barrier, n_dp - 1 + Y * (n_seq - 1))

    def wrows(first, count):
        return wbuf.at[pl.ds(pl.multiple_of(first * rows, 16), count * rows), :]

    for b in range(HALF):
        push(
            weight.at[:, pl.ds(b * cols, cols)],
            wrows(d, 1),
            WY + slot,
            z * Y + HALF * c + b,
            CORES * x + core,
        )

    def send_a(i, carry):
        p = lax.rem(d + i, n_dp)
        remote(a_send.at[p], a_recv.at[d], A, p, j)
        return carry

    lax.fori_loop(1, n_dp, send_a, 0)

    for copy in loads[3:]:
        copy.wait()

    @pl.when(own)
    def _():
        for py in range(Y):

            @pl.when(py == y)
            def _():
                pltpu.make_async_copy(own_mods, mods.at[slot], recv.at[MOD]).start()

            @pl.when(py != y)
            def _():
                pltpu.make_async_remote_copy(
                    src_ref=own_mods,
                    dst_ref=mods.at[slot],
                    send_sem=mod_send.at[py],
                    recv_sem=recv.at[MOD],
                    device_id=(z * Y + py, j),
                    device_id_type=MESH,
                ).start()

    def lanes(i, count):
        return pl.ds(pl.multiple_of(i * count, LANES), count)

    def chip_of(i):
        h = lax.rem(head + i, heads)
        return h, z * Y + lax.rem(h, Y), CORES * lax.div(h, Y) + core

    def send_text(i, how):
        h, dp, seq = chip_of(i)
        here = pl.ds(pl.multiple_of(j * tloc, 16), tloc)
        how(text.at[:, lanes(h, cols)], qkv.at[slot, here, :], TXT, dp, seq)

    def send_grad(i, how):
        h, dp, seq = chip_of(i)
        here = pl.ds(pl.multiple_of(j * tloc, 16), tloc)
        how(grad_txt.at[:, lanes(h, HD)], dout.at[slot, here, :], DTXT, dp, seq)
        here = pl.ds(pl.multiple_of(texts + j * local, 16), local)
        how(grad_img.at[:, lanes(h, HD)], dout.at[slot, here, :], DIMG, dp, seq)

    embed_f = embed[...].astype(F32)
    embed_centred = embed_f - jnp.sum(embed_f, axis=1, keepdims=True) * (1.0 / width)

    def piece(pz, p):
        return wrows(pz * Y + c * HALF + p, 1)

    def hop(pz, p, to, sems, step):
        pltpu.make_async_remote_copy(
            src_ref=piece(pz, p),
            dst_ref=piece(pz, p),
            send_sem=ring_send,
            recv_sem=sems.at[step, p],
            device_id=(to * Y + y, j),
            device_id_type=MESH,
        ).start()

    def landed(pz, p, sems, step):
        pltpu.make_async_copy(piece(pz, p), piece(pz, p), sems.at[step, p]).wait()

    def to_sibling(pz, p):
        remote(piece(pz, p), piece(pz, p), SIB, d, CORES * x + (1 - c))

    up, down = lax.rem(z + 1, n_z), lax.rem(z + n_z - 1, n_z)
    last = n_z // 2 - 1
    for p in range(HALF):
        arrived(piece(z, p), WY + p)
        hop(z, p, up, ring_right, 0)
        hop(z, p, down, ring_left, 0)
        to_sibling(z, p)

    def ring_step(step):
        from_left = lax.rem(z + n_z - 1 - step, n_z)
        from_right = lax.rem(z + 1 + step, n_z)
        for p in range(HALF):
            if step < last:
                landed(from_left, p, ring_right, step)
                if step + 1 < last or p == 0:
                    hop(from_left, p, up, ring_right, step + 1)
                landed(from_right, p, ring_left, step)
                if step + 1 < last or p == 1:
                    hop(from_right, p, down, ring_left, step + 1)
                to_sibling(from_left, p)
                to_sibling(from_right, p)
            else:
                landed(from_left, p, (ring_right, ring_left)[p], step)
                to_sibling(from_left, p)

    each(send_text)

    arrived(a_recv.at[pl.ds(0, n_dp - 1)], A)
    shape = (local, local)
    r, k = iota(shape, 0), iota(shape, 1)
    gather = jnp.logical_and(over(r, block) == within(k, n_dp), within(r, block) == over(k, n_dp))
    gather = gather.astype(F32).astype(BF)
    stacked = jnp.concatenate([a_recv[:, t, :] for t in range(block)], axis=0)
    mine = mm(gather, stacked.astype(BF))
    xs = mm(mine[:, :channels].astype(BF), embed[...])
    centred = xs - jnp.sum(xs, axis=1, keepdims=True) * (1.0 / width)
    inv = lax.rsqrt(jnp.sum(centred * centred, axis=1, keepdims=True) * (1.0 / width) + EPS)
    xhat = (centred * inv).astype(BF)
    inv_high, inv_low = split(inv)
    lane = iota((local, LANES), 1)
    mine = jnp.where(lane == INV_HIGH, inv_high.astype(F32), mine)
    mine = jnp.where(lane == INV_LOW, inv_low.astype(F32), mine)
    mine = jnp.where(lane == TEXT_LEN, text_len[0].astype(F32), mine)
    own_tok[...] = mine.astype(BF)
    half = local // 2
    only = jnp.where(lane < channels, mine, 0.0)
    own_pack[:half] = (only[:half] + pltpu.roll(only[half:], channels, 1)).astype(BF)
    flag = (iota((16, LANES), 1) == iota((16, LANES), 0) + LIVE).astype(F32).astype(BF)
    own_pack[half:] = jnp.zeros((16, LANES), BF)
    own_pack[half:, :local] = mm_nt(flag, own_tok[...]).astype(BF)

    def send_tok(i, how):
        h, dp, seq = chip_of(i)
        how(own_pack, tokp.at[slot * n_seq + j], TOK, dp, seq)

    each(send_tok)
    ring_step(0)
    back[...] = jnp.zeros_like(back)
    back[:, :channels] = mm_nt(xhat, embed[...])

    arrived(mods, MOD)
    tail = jnp.zeros((16, width), F32)
    at = iota((16, width), 0)
    for u in range(HALF):
        high, low = split(embed_centred * (1.0 + mods[u, 0]))
        amat[u * channels : (u + 1) * channels, :] = high
        amat[(HALF + u) * channels : (HALF + u + 1) * channels, :] = low
        high, low = split(mods[u, 1])
        tail = jnp.where(at == u, high.astype(F32), tail)
        tail = jnp.where(at == HALF + u, low.astype(F32), tail)
        high, low = split((1.0 + mods[u, 0]) * (1.0 / width))
        tail = jnp.where(at == 2 * HALF + u, high.astype(F32), tail)
        tail = jnp.where(at == 3 * HALF + u, low.astype(F32), tail)
    amat[2 * HALF * channels :, :] = tail.astype(BF)
    centred_b[...] = embed_centred.astype(BF)

    for step in range(1, last):
        ring_step(step)
    each(send_grad)

    arrived(tokp, TOK)
    half = local // 2
    low_lane = iota((half, LANES), 1) < channels
    for i in range(heads):
        packed = tokp[i, :half].astype(F32)
        flags = mm_tn(tokp[i, half:], flag)
        first = jnp.where(low_lane, packed, 0.0) + flags[:half]
        second = jnp.where(low_lane, pltpu.roll(packed, channels, 1), 0.0) + flags[half:local]
        tok[i * local : i * local + half] = first.astype(BF)
        tok[i * local + half : (i + 1) * local] = second.astype(BF)

    lane = iota((images, LANES), 1)
    tlane = iota((texts, LANES), 1)
    trow = iota((texts, LANES), 0)
    for u in range(HALF):
        tk = tok[u * images : (u + 1) * images]
        tf = tk.astype(F32)
        length = tf[0:1, TEXT_LEN : TEXT_LEN + 1]
        kaug[u, texts:, HD:] = jnp.where(lane == LIVE, (tf - 1.0) * 1e30, 0.0).astype(BF)
        bad = jnp.logical_and(tlane == LIVE, trow.astype(F32) >= length)
        kaug[u, :texts, HD:] = jnp.where(bad, -1e30, 0.0).astype(BF)
        vaug[u, :, HD:] = jnp.ones((total, LANES), BF)
        vt[u, HD:, :] = jnp.ones((16, total), BF)
        flag_rows = mm_nt(flag, tk)
        inv_row[u] = flag_rows[1:2] + flag_rows[2:3]
        scaled_t[u] = (tf.T * inv_row[u]).astype(BF)
        valid_row[u, :, texts:] = flag_rows[0:1]
        valid_row[u, :, :texts] = (iota((1, texts), 1).astype(F32) < length).astype(F32)
    arrived(qkv.at[:, pl.ds(0, texts), :], TXT)
    for u in range(HALF):
        kaug[u, :texts, :HD] = qkv[u, :texts, HD : 2 * HD]
        vaug[u, :texts, :HD] = qkv[u, :texts, 2 * HD :]
        kt[u, :, :texts] = qkv[u, :texts, HD : 2 * HD].T
        vt[u, :HD, :texts] = qkv[u, :texts, 2 * HD :].T

    ring_step(last)
    arrived(wbuf.at[pl.ds(0, n_z * HALF * rows), :], SIB)
    product = mm(amat[...], wbuf[...])
    base = 2 * HALF * channels
    for u in range(HALF):
        sums = (
            product[u * channels : (u + 1) * channels]
            + product[(HALF + u) * channels : (HALF + u + 1) * channels]
        )
        sums = jnp.concatenate([sums, jnp.zeros((LANES - channels, cols), F32)], axis=0)
        mixed[u, 0], mixed[u, 1] = split(sums)
        mixed_t[u, 0], mixed_t[u, 1] = split(sums.T)
        const = product[base + u : base + u + 1] + product[base + HALF + u : base + HALF + u + 1]
        wbar[u] = (
            product[base + 2 * HALF + u : base + 2 * HALF + u + 1]
            + product[base + 3 * HALF + u : base + 3 * HALF + u + 1]
        )
        const_t = jnp.broadcast_to(const[:, HD:], (LANES, 2 * HD)).T
        tk = tok[u * images : (u + 1) * images]
        tf = tk.astype(F32)
        invs = tf[:, INV_HIGH : INV_HIGH + 1] + tf[:, INV_LOW : INV_LOW + 1]
        got = ((mm(tk, mixed[u, 0]) + mm(tk, mixed[u, 1])) * invs + const).astype(BF)
        qkv[u, texts:, :HD] = got[:, :HD]
        kaug[u, texts:, :HD] = got[:, HD : 2 * HD]
        vaug[u, texts:, :HD] = got[:, 2 * HD :]
        got = mm_nt(mixed_t[u, 0, HD:], tk) + mm_nt(mixed_t[u, 1, HD:], tk)
        got = (got * inv_row[u] + const_t[:, 0:1]).astype(BF)
        kt[u, :, texts:] = got[:HD]
        vt[u, :HD, texts:] = got[HD:]

    factor = 1.0 / math.sqrt(HD)
    log2e = factor * math.log2(math.e)

    for u in range(HALF):
        query = qkv[u, :, :HD]
        ones = (iota((total, LANES), 1) == LIVE).astype(F32).astype(BF)
        score = mm_nt(kaug[u], jnp.concatenate([query, ones], axis=1))
        top = jnp.max(score, axis=0, keepdims=True)
        expo = jnp.exp2((score - top) * log2e).astype(BF)
        got = mm(vt[u], expo)
        share = valid_row[u] / got[HD : HD + 1]
        out_buf[u] = (got[:HD] * share).T.astype(BF)
        sbuf[u] = jnp.broadcast_to(share, (LANES, total)).T
        ebuf[u] = expo

    def slab(i):
        u = lax.rem(slot + lax.div(i, n_seq), HALF)
        return u, lax.rem(j + lax.rem(i, n_seq), n_seq)

    def send_out(i, how):
        u, s = slab(i)
        dp = z * Y + c * HALF + u
        rows_of = pl.ds(pl.multiple_of(texts + s * local, 16), local)
        how(out_buf.at[u, rows_of, :], img_recv.at[:, lanes(head, HD)], OIMG, dp, s)
        rows_of = pl.ds(pl.multiple_of(s * tloc, 16), tloc)
        how(out_buf.at[u, rows_of, :], txt_recv.at[:, lanes(head, HD)], OTXT, dp, s)

    each(send_out)

    arrived(dout.at[:, pl.ds(texts, images), :], DIMG)
    arrived(dout.at[:, pl.ds(0, texts), :], DTXT)
    lane = iota((total, LANES), 1)
    for u in range(HALF):
        expo, share = ebuf[u], sbuf[u]
        up = dout[u].astype(F32)
        delta = jnp.sum(up * out_buf[u].astype(F32), axis=1, keepdims=True) * share
        scaled = (up * share).astype(BF)
        high, low = split(delta)
        tail = jnp.where(lane == 0, -high.astype(F32), 0.0)
        tail = jnp.where(lane == 1, -low.astype(F32), tail).astype(BF)
        dprob = mm_nt(vaug[u], jnp.concatenate([scaled, tail], axis=1))
        dscore = expo * dprob.astype(BF)
        dqkv[u, :, 2 * HD :] = mm(expo, scaled).astype(BF)
        dqkv[u, :, HD : 2 * HD] = (mm(dscore, qkv[u, :, :HD]) * factor).astype(BF)
        dqkv[u, :, :HD] = (mm(kt[u], dscore) * factor).T.astype(BF)

    gram = jnp.zeros((LANES, LANES), F32)
    seen = []
    for u in range(HALF):
        grad = dqkv[u, texts:, :]
        seen.append(mm(scaled_t[u], grad)[:channels])
        scaled = scaled_t[u].astype(F32)
        project = jnp.sum(scaled * mm_nt(mixed[u, 0], grad), axis=0, keepdims=True)
        project = project * (inv_row[u] * (1.0 / width))
        gram += mm((scaled * project).astype(BF), tok[u * images : (u + 1) * images])
    seen = jnp.concatenate(seen, axis=0).astype(BF)
    gram = gram[:channels, :channels].astype(BF)
    average = jnp.zeros((channels, 1), F32)
    for u in range(HALF):
        mine = seen[u * channels : (u + 1) * channels].astype(F32)
        average += jnp.sum(mine * wbar[u], axis=1, keepdims=True)

    er, ec = channels // Y, width // n_seq

    me = y * n_seq + j
    plane = Y * n_seq

    def weight_block(i, carry):
        q = lax.rem(j + i, n_seq)
        at = lanes(q, ec)
        spread = mm_nt(seen, wbuf[pl.ds(pl.multiple_of(q * ec, LANES), ec), :])
        part = -mm(gram, centred_b[:, at]) - average
        for u in range(HALF):
            part += spread[u * channels : (u + 1) * channels] * (1.0 + mods[u, 0, :, at])
        for py in range(Y):
            t_send[py * n_seq + q] = part[py * er : (py + 1) * er].astype(BF)

            @pl.when(jnp.logical_not(jnp.logical_and(py == y, q == j)))
            def _():
                remote(t_send.at[py * n_seq + q], h1.at[me], H1, z * Y + py, q)

        return carry

    lax.fori_loop(0, n_seq, weight_block, 0)
    h1[me] = t_send[me]

    for u in range(HALF):
        part = mm(dqkv[u, texts:, :], mixed_t[u, 0])
        for s in range(n_seq):
            own_part = part[s * local : (s + 1) * local]
            packed = own_part[: local // 2] + pltpu.roll(own_part[local // 2 :], channels, 1)
            f_send[u * n_seq + s] = packed.astype(BF)

    def send_feat(i, how):
        u, s = slab(i)
        how(f_send.at[u * n_seq + s], f_recv.at[head], FEAT, z * Y + c * HALF + u, s)

    each(send_feat)

    arrived(h1.at[pl.ds(0, plane - 1)], H1)
    h2[z] = jnp.sum(h1[...].astype(F32), axis=0).astype(BF)

    def send_h2(i, carry):
        p = lax.rem(z + i, n_z)
        remote(h2.at[z], h2.at[z], H2, p * Y + y, j)
        return carry

    lax.fori_loop(1, n_z, send_h2, 0)
    arrived(f_recv, FEAT)
    half = local // 2
    packed = jnp.sum(f_recv[...].astype(F32), axis=0)
    lane = iota((half, LANES), 1)
    feat = jnp.concatenate(
        [
            jnp.where(lane < channels, packed, 0.0),
            jnp.where(lane < channels, pltpu.roll(packed, channels, 1), 0.0),
        ],
        axis=0,
    )
    mine = own_tok[...].astype(F32)
    inv = mine[:, INV_HIGH : INV_HIGH + 1] + mine[:, INV_LOW : INV_LOW + 1]
    project = jnp.sum(mine * feat, axis=1, keepdims=True) * (inv * (1.0 / width))
    ddeq = inv * (feat - back[...] * project)
    spread = mm_tn(gather, ddeq.astype(BF))
    for t in range(block):
        g_send[:, t, :] = spread[t * n_dp : (t + 1) * n_dp]

    def send_g(i, carry):
        p = lax.rem(d + i, n_dp)
        remote(g_send.at[p], g_recv.at[d], G, p, j)
        return carry

    lax.fori_loop(1, n_dp, send_g, 0)
    g_recv[d] = g_send[d]

    arrived(h2.at[pl.ds(0, n_z - 1)], H2)
    h3[me] = jnp.sum(h2[...].astype(F32), axis=0).astype(BF)

    def send_h3(i, carry):
        py, pj = plane_peer(i)

        @pl.when(i != Y // 2 * n_seq)
        def _():
            remote(h3.at[me], h3.at[me], H3, z * Y + py, pj)

        return carry

    lax.fori_loop(0, plane, send_h3, 0)

    arrived(img_recv, OIMG)
    arrived(txt_recv, OTXT)
    stores = [
        pltpu.make_async_copy(img_recv, out_img, store.at[0]),
        pltpu.make_async_copy(txt_recv, out_txt, store.at[1]),
    ]
    for copy in stores:
        copy.start()

    arrived(g_recv.at[pl.ds(0, n_dp - 1)], G)
    blocks = codes.shape[0]
    chosen = (slot_row[...] == iota((blocks, n_dp), 0)).astype(F32).astype(BF)
    pad_scale = mm(scales[...], pad_eye)
    codes_of = [mm(chosen, g_recv[:, t, :].astype(BF)) * pad_scale for t in range(block)]
    for t in range(0, block, 2):
        code_out[:, 0, t // 2 * LANES : (t // 2 + 1) * LANES] = codes_of[t] + pltpu.roll(
            codes_of[t + 1], channels, 1
        )

    left_here(a_send.at[pl.ds(0, n_dp - 1)], A)
    sent(weight.at[:, pl.ds(0, (HALF - 1) * cols)], weight.at[:, pl.ds(0, HALF * cols)], WY + slot)

    @pl.when(own)
    def _():
        for py in range(Y):

            @pl.when(py != y)
            def _():
                pltpu.make_async_copy(own_mods, own_mods, mod_send.at[py]).wait()

    few = heads - 1
    sent(text.at[:, pl.ds(0, few * cols)], text, TXT)
    sent(grad_txt.at[:, pl.ds(0, few * HD)], grad_txt, DTXT)
    sent(grad_img.at[:, pl.ds(0, few * HD)], grad_img, DIMG)
    sent(tokp.at[pl.ds(0, few)], tokp, TOK)
    left_here(wbuf.at[pl.ds(0, n_z * HALF * rows), :], SIB)
    gone = wbuf.at[pl.ds(0, (n_z - 1) * HALF * rows), :]
    pltpu.make_async_copy(gone, gone, ring_send).wait()
    sent(img_recv.at[:, pl.ds(0, few * HD)], img_recv, OIMG)
    sent(txt_recv.at[:, pl.ds(0, few * HD)], txt_recv, OTXT)
    sent(f_send.at[pl.ds(0, few)], f_send, FEAT)
    left_here(g_send.at[pl.ds(0, n_dp - 1)], G)
    left_here(h1.at[pl.ds(0, plane - 1)], H1)
    left_here(h2.at[pl.ds(0, n_z - 1)], H2)
    left_here(h1.at[pl.ds(0, plane - 1)], H3)

    arrived(h1.at[pl.ds(0, plane - 1)], H3)
    for py in range(Y):
        for q in range(n_seq):
            whole[py * er : (py + 1) * er, q * ec : (q + 1) * ec] = h3[py * n_seq + q]
    to_hbm = pltpu.make_async_copy(whole, embed_out, store.at[2])
    to_hbm.start()
    to_hbm.wait()
    for copy in stores:
        copy.wait()


def finish(*refs):
    sources, results, held = refs[:4], refs[4:8], refs[8:12]
    wide, came, went = refs[12:]
    inward = [
        pltpu.make_async_copy(sources[i], held[i], came.at[i]) for i in (3, 0, 1, 2)
    ]
    for copy in inward:
        copy.start()
    inward[0].wait()
    wide[...] = held[3][...].astype(F32)
    last = pltpu.make_async_copy(wide, results[3], went.at[3])
    last.start()
    outward = [pltpu.make_async_copy(held[i], results[i], went.at[i]) for i in range(3)]
    for before, copy in zip(inward[1:], outward):
        before.wait()
        copy.start()
    for copy in outward:
        copy.wait()
    last.wait()


def per_device(
    n_dp,
    n_seq,
    latent_codes,
    latent_scales,
    send_list,
    embed_weight,
    modulation_offset,
    mod_scale,
    qkv_weight,
    text_qkv,
    text_len,
    out_grad_img,
    out_grad_txt,
):
    codes, scales = latent_codes[0, 0], latent_scales[0, 0]
    slots = send_list[0, 0]
    channels, width = embed_weight.shape
    local, tloc = out_grad_img.shape[1], out_grad_txt.shape[1]
    images, texts = local * n_seq, tloc * n_seq
    total = images + texts
    heads = Y * n_seq // CORES
    cols = 3 * HD
    n_z = n_dp // Y
    er, ec = channels // Y, width // n_seq
    vmem, hbm = pl.BlockSpec(memory_space=pltpu.VMEM), pl.BlockSpec(memory_space=pltpu.HBM)
    block = codes.shape[1]
    scratch = [
        pltpu.SMEM((1,), jnp.int32),
        pltpu.VMEM(codes.shape, BF),
        pltpu.VMEM(scales.shape, BF),
        pltpu.VMEM((1, n_dp), jnp.int32),
        pltpu.VMEM((channels, width), BF),
        pltpu.VMEM((n_dp, 4, LANES), F32),
        pltpu.VMEM((n_dp, 4, LANES), F32),
        pltpu.VMEM((local, LANES), BF),
        pltpu.VMEM((local // 2 + 16, LANES), BF),
        pltpu.VMEM((heads, local // 2 + 16, LANES), BF),
        pltpu.VMEM((2, 1, width), F32),
        pltpu.VMEM((HALF * images, LANES), BF),
        pltpu.VMEM((HALF, 2, 1, width), F32),
        pltpu.VMEM((width, cols), BF),
        pltpu.VMEM((2 * HALF * channels + 16, width), BF),
        pltpu.VMEM((HALF, 2, LANES, cols), BF),
        pltpu.VMEM((HALF, total, cols), BF),
        pltpu.VMEM((HALF, total, HD), BF),
        pltpu.VMEM((HALF, total, 2 * HD), BF),
        pltpu.VMEM((HALF, total, 2 * HD), BF),
        pltpu.VMEM((HALF, HD, total), BF),
        pltpu.VMEM((HALF, HD + 16, total), BF),
        pltpu.VMEM((HALF, total, total), BF),
        pltpu.VMEM((HALF, total, LANES), F32),
        pltpu.VMEM((HALF, 2, cols, LANES), BF),
        pltpu.VMEM((HALF, 1, cols), F32),
        pltpu.VMEM((channels, width), BF),
        pltpu.VMEM((HALF, 1, images), F32),
        pltpu.VMEM((HALF, LANES, images), BF),
        pltpu.VMEM((HALF, 1, total), F32),
        pltpu.VMEM((HALF, total, HD), BF),
        pltpu.VMEM((local, heads * HD), BF),
        pltpu.VMEM((tloc, heads * HD), BF),
        pltpu.VMEM((HALF, total, cols), BF),
        pltpu.VMEM((heads, local // 2, LANES), BF),
        pltpu.VMEM((heads, local // 2, LANES), BF),
        pltpu.VMEM((local, LANES), F32),
        pltpu.VMEM((n_dp, 4, LANES), F32),
        pltpu.VMEM((n_dp, 4, LANES), F32),
        pltpu.VMEM((Y * n_seq, er, ec), BF),
        pltpu.VMEM((Y * n_seq, er, ec), BF),
        pltpu.VMEM((n_z, er, ec), BF),
        pltpu.VMEM((Y * n_seq, er, ec), BF),
        pltpu.VMEM((channels, width), BF),
        pltpu.SemaphoreType.DMA((7,)),
        pltpu.SemaphoreType.DMA((3,)),
        pltpu.SemaphoreType.DMA((16,)),
        pltpu.SemaphoreType.DMA((16,)),
        pltpu.SemaphoreType.DMA((Y,)),
        pltpu.SemaphoreType.DMA((n_z // 2, HALF)),
        pltpu.SemaphoreType.DMA((n_z // 2, HALF)),
        pltpu.SemaphoreType.DMA,
    ]
    out = pl.pallas_call(
        functools.partial(kernel, n_dp, n_seq),
        out_shape=(
            jax.ShapeDtypeStruct((local, heads * HD), BF),
            jax.ShapeDtypeStruct((tloc, heads * HD), BF),
            jax.ShapeDtypeStruct((codes.shape[0], 1, block), F32),
            jax.ShapeDtypeStruct((channels, width), BF),
        ),
        in_specs=[hbm] * 11,
        out_specs=(hbm, hbm, vmem, hbm),
        scratch_shapes=scratch,
        compiler_params=pltpu.CompilerParams(
            collective_id=0, has_side_effects=True, vmem_limit_bytes=61 * 1024 * 1024
        ),
    )(
        text_len,
        codes,
        scales,
        slots[None, :],
        embed_weight,
        modulation_offset,
        mod_scale,
        qkv_weight,
        text_qkv[0],
        out_grad_img[0],
        out_grad_txt[0],
    )
    img, txt, code, grad = pl.pallas_call(
        finish,
        out_shape=tuple(
            jax.ShapeDtypeStruct(part.shape, kind) for part, kind in zip(out, (BF, BF, F32, F32))
        ),
        in_specs=[hbm] * 4,
        out_specs=(hbm,) * 4,
        scratch_shapes=[pltpu.VMEM(part.shape, part.dtype) for part in out]
        + [
            pltpu.VMEM((channels, width), F32),
            pltpu.SemaphoreType.DMA((4,)),
            pltpu.SemaphoreType.DMA((4,)),
        ],
        compiler_params=pltpu.CompilerParams(vmem_limit_bytes=61 * 1024 * 1024),
    )(*out)
    return img[None], txt[None], code[:, 0][None, None], grad


def solution(mesh):
    return jax.shard_map(
        functools.partial(per_device, mesh.shape["dp"], mesh.shape["seq"]),
        mesh=mesh,
        in_specs=(
            P("dp", "seq", None, None),
            P("dp", "seq", None, None),
            P("dp", "seq", None),
            P(),
            P("dp", None),
            P("dp", None),
            P("dp", "seq"),
            P("dp", "seq", None),
            P("dp"),
            P("dp", "seq", None),
            P("dp", "seq", None),
        ),
        out_specs=(P("dp", "seq", None), P("dp", "seq", None), P("dp", "seq", None, None), P()),
        check_vma=False,
    )
```

```python
import functools
import math

import jax
import jax.numpy as jnp
from jax import lax
from jax.experimental import pallas as pl
from jax.experimental.pallas import tpu as pltpu
from jax.sharding import PartitionSpec as P

MESH = pl.DeviceIdType.MESH
CUT = 99
BF, F32 = jnp.bfloat16, jnp.float32
HD = 128
LANES = 128
EPS = 1e-06
Y = 4
CORES = 2
HALF = Y // CORES
LIVE, INV_HIGH, INV_LOW, TEXT_LEN = 64, 65, 66, 67


def mm(a, b):
    return jnp.dot(a, b, preferred_element_type=F32)


def mm_nt(a, b):
    return lax.dot_general(a, b, (((1,), (1,)), ((), ())), preferred_element_type=F32)


def mm_tn(a, b):
    return lax.dot_general(a, b, (((0,), (0,)), ((), ())), preferred_element_type=F32)


def iota(shape, dim):
    return lax.broadcasted_iota(jnp.int32, shape, dim)


def over(value, power):
    return lax.shift_right_logical(value, jnp.full_like(value, power.bit_length() - 1))


def within(value, power):
    return jnp.bitwise_and(value, power - 1)


def split(value):
    high = value.astype(BF)
    return high, (value - high.astype(F32)).astype(BF)


def kernel(
    n_dp,
    n_seq,
    text_len_hbm,
    codes_hbm,
    scales_hbm,
    slots_hbm,
    embed_hbm,
    shift_hbm,
    scale_hbm,
    weight,
    text,
    grad_img,
    grad_txt,
    out_img,
    out_txt,
    code_out,
    embed_out,
    text_len,
    codes,
    scales,
    slot_row,
    embed,
    a_send,
    a_recv,
    own_tok,
    own_pack,
    tokp,
    own_mods,
    tok,
    mods,
    wbuf,
    amat,
    mixed,
    qkv,
    dout,
    kaug,
    vaug,
    kt,
    vt,
    ebuf,
    sbuf,
    mixed_t,
    wbar,
    centred_b,
    inv_row,
    scaled_t,
    valid_row,
    out_buf,
    img_recv,
    txt_recv,
    dqkv,
    f_send,
    f_recv,
    back,
    g_send,
    g_recv,
    t_send,
    h1,
    h2,
    h3,
    whole,
    load,
    store,
    send,
    recv,
    mod_send,
    ring_right,
    ring_left,
    ring_send,
):
    d, j = lax.axis_index("dp"), lax.axis_index("seq")
    z, y = lax.div(d, Y), lax.rem(d, Y)
    x, c = lax.div(j, CORES), lax.rem(j, CORES)
    slot, core = lax.rem(y, HALF), lax.div(y, HALF)
    own = core == c
    head = Y * x + y
    n_z, heads = n_dp // Y, Y * n_seq // CORES
    channels, width = embed_hbm.shape
    rows = weight.shape[0]
    local = grad_img.shape[0]
    tloc = grad_txt.shape[0]
    images, texts = local * n_seq, tloc * n_seq
    total = images + texts
    block = local // n_dp
    cols = 3 * HD

    def same(dp, seq):
        return jnp.logical_and(dp == d, seq == j)

    def remote(src, dst, k, dp, seq):
        pltpu.make_async_remote_copy(
            src_ref=src,
            dst_ref=dst,
            send_sem=send.at[k],
            recv_sem=recv.at[k],
            device_id=(dp, seq),
            device_id_type=MESH,
        ).start()

    def push(src, dst, k, dp, seq):
        @pl.when(same(dp, seq))
        def _():
            pltpu.make_async_copy(src, dst, recv.at[k]).start()

        @pl.when(jnp.logical_not(same(dp, seq)))
        def _():
            remote(src, dst, k, dp, seq)

    def each(send_one):
        send_one(0, push)

        def others(i, carry):
            send_one(i, remote)
            return carry

        lax.fori_loop(1, heads, others, 0)

    def arrived(ref, k):
        pltpu.make_async_copy(ref, ref, recv.at[k]).wait()

    def left_here(ref, k):
        pltpu.make_async_copy(ref, ref, send.at[k]).wait()

    def sent(some, whole, k):
        @pl.when(own)
        def _():
            left_here(some, k)

        @pl.when(jnp.logical_not(own))
        def _():
            left_here(whole, k)

    A, MOD, TXT, DIMG, TOK, SIB, OIMG, OTXT, FEAT, G, H1, H2, H3, DTXT, WY = range(15)

    def plane_peer(i):
        py = lax.rem(y + lax.div(i, n_seq) + Y // 2, Y)
        return py, lax.rem(j + lax.rem(i, n_seq), n_seq)

    loads = [
        pltpu.make_async_copy(src, dst, load.at[i])
        for i, (src, dst) in enumerate(
            (
                (slots_hbm, slot_row),
                (codes_hbm, codes),
                (scales_hbm, scales),
                (embed_hbm, embed),
                (scale_hbm, own_mods.at[0]),
                (shift_hbm, own_mods.at[1]),
                (text_len_hbm, text_len),
            )
        )
    ]
    for copy in loads:
        copy.start()

    barrier = pltpu.get_barrier_semaphore()

    def greet_dp(i, carry):
        pl.semaphore_signal(
            barrier, inc=1, device_id=(lax.rem(d + i, n_dp), j), device_id_type=MESH
        )
        return carry

    lax.fori_loop(1, n_dp, greet_dp, 0)

    def greet_plane(i, carry):
        py = lax.rem(y + lax.div(i, n_seq - 1), Y)
        pj = lax.rem(j + 1 + lax.rem(i, n_seq - 1), n_seq)
        pl.semaphore_signal(barrier, inc=1, device_id=(z * Y + py, pj), device_id_type=MESH)
        return carry

    lax.fori_loop(0, Y * (n_seq - 1), greet_plane, 0)

    for copy in loads[:3]:
        copy.wait()
    square = (n_dp, n_dp)
    diagonal = iota(square, 0) == iota(square, 1)
    slot_col = jnp.sum(
        jnp.where(diagonal, slot_row[...].astype(F32), 0.0), axis=1, keepdims=True
    ).astype(jnp.int32)
    pick = (slot_col == iota((n_dp, codes.shape[0]), 1)).astype(F32).astype(BF)
    used = jnp.sum(pick.astype(F32), axis=1, keepdims=True)
    pad_eye = (iota((channels, LANES), 0) == iota((channels, LANES), 1)).astype(F32).astype(BF)
    lane = iota((n_dp, LANES), 1)
    picked_scale = mm(mm(pick, scales[...]).astype(BF), pad_eye)
    picked_code = mm(pick, codes[...])
    for t in range(block):
        part = picked_code[:, (t // 2) * LANES : (t // 2 + 1) * LANES]
        if t % 2:
            part = pltpu.roll(part, channels, 1)
        part = (part * picked_scale).astype(BF).astype(F32)
        a_send[:, t, :] = jnp.where(lane == LIVE, used, part)
    a_recv[d] = a_send[d]

    pl.semaphore_wait(barrier, n_dp - 1 + Y * (n_seq - 1))

    def wrows(first, count):
        return wbuf.at[pl.ds(pl.multiple_of(first * rows, 16), count * rows), :]

    for b in range(HALF):
        push(
            weight.at[:, pl.ds(b * cols, cols)],
            wrows(d, 1),
            WY + slot,
            z * Y + HALF * c + b,
            CORES * x + core,
        )

    def send_a(i, carry):
        p = lax.rem(d + i, n_dp)
        remote(a_send.at[p], a_recv.at[d], A, p, j)
        return carry

    lax.fori_loop(1, n_dp, send_a, 0)

    for copy in loads[3:]:
        copy.wait()

    @pl.when(own)
    def _():
        for py in range(Y):

            @pl.when(py == y)
            def _():
                pltpu.make_async_copy(own_mods, mods.at[slot], recv.at[MOD]).start()

            @pl.when(py != y)
            def _():
                pltpu.make_async_remote_copy(
                    src_ref=own_mods,
                    dst_ref=mods.at[slot],
                    send_sem=mod_send.at[py],
                    recv_sem=recv.at[MOD],
                    device_id=(z * Y + py, j),
                    device_id_type=MESH,
                ).start()

    def lanes(i, count):
        return pl.ds(pl.multiple_of(i * count, LANES), count)

    def chip_of(i):
        h = lax.rem(head + i, heads)
        return h, z * Y + lax.rem(h, Y), CORES * lax.div(h, Y) + core

    def send_text(i, how):
        h, dp, seq = chip_of(i)
        here = pl.ds(pl.multiple_of(j * tloc, 16), tloc)
        how(text.at[:, lanes(h, cols)], qkv.at[slot, here, :], TXT, dp, seq)

    def send_grad(i, how):
        h, dp, seq = chip_of(i)
        here = pl.ds(pl.multiple_of(j * tloc, 16), tloc)
        how(grad_txt.at[:, lanes(h, HD)], dout.at[slot, here, :], DTXT, dp, seq)
        here = pl.ds(pl.multiple_of(texts + j * local, 16), local)
        how(grad_img.at[:, lanes(h, HD)], dout.at[slot, here, :], DIMG, dp, seq)

    embed_f = embed[...].astype(F32)
    embed_centred = embed_f - jnp.sum(embed_f, axis=1, keepdims=True) * (1.0 / width)

    def piece(pz, p):
        return wrows(pz * Y + c * HALF + p, 1)

    def hop(pz, p, to, sems, step):
        pltpu.make_async_remote_copy(
            src_ref=piece(pz, p),
            dst_ref=piece(pz, p),
            send_sem=ring_send,
            recv_sem=sems.at[step, p],
            device_id=(to * Y + y, j),
            device_id_type=MESH,
        ).start()

    def landed(pz, p, sems, step):
        pltpu.make_async_copy(piece(pz, p), piece(pz, p), sems.at[step, p]).wait()

    def to_sibling(pz, p):
        remote(piece(pz, p), piece(pz, p), SIB, d, CORES * x + (1 - c))

    up, down = lax.rem(z + 1, n_z), lax.rem(z + n_z - 1, n_z)
    last = n_z // 2 - 1
    for p in range(HALF):
        arrived(piece(z, p), WY + p)
        hop(z, p, up, ring_right, 0)
        hop(z, p, down, ring_left, 0)
        to_sibling(z, p)

    def ring_step(step):
        from_left = lax.rem(z + n_z - 1 - step, n_z)
        from_right = lax.rem(z + 1 + step, n_z)
        for p in range(HALF):
            if step < last:
                landed(from_left, p, ring_right, step)
                if step + 1 < last or p == 0:
                    hop(from_left, p, up, ring_right, step + 1)
                landed(from_right, p, ring_left, step)
                if step + 1 < last or p == 1:
                    hop(from_right, p, down, ring_left, step + 1)
                to_sibling(from_left, p)
                to_sibling(from_right, p)
            else:
                landed(from_left, p, (ring_right, ring_left)[p], step)
                to_sibling(from_left, p)


    arrived(a_recv.at[pl.ds(0, n_dp - 1)], A)
    shape = (local, local)
    r, k = iota(shape, 0), iota(shape, 1)
    gather = jnp.logical_and(over(r, block) == within(k, n_dp), within(r, block) == over(k, n_dp))
    gather = gather.astype(F32).astype(BF)
    stacked = jnp.concatenate([a_recv[:, t, :] for t in range(block)], axis=0)
    mine = mm(gather, stacked.astype(BF))
    xs = mm(mine[:, :channels].astype(BF), embed[...])
    centred = xs - jnp.sum(xs, axis=1, keepdims=True) * (1.0 / width)
    inv = lax.rsqrt(jnp.sum(centred * centred, axis=1, keepdims=True) * (1.0 / width) + EPS)
    xhat = (centred * inv).astype(BF)
    inv_high, inv_low = split(inv)
    lane = iota((local, LANES), 1)
    mine = jnp.where(lane == INV_HIGH, inv_high.astype(F32), mine)
    mine = jnp.where(lane == INV_LOW, inv_low.astype(F32), mine)
    mine = jnp.where(lane == TEXT_LEN, text_len[0].astype(F32), mine)
    own_tok[...] = mine.astype(BF)
    half = local // 2
    only = jnp.where(lane < channels, mine, 0.0)
    own_pack[:half] = (only[:half] + pltpu.roll(only[half:], channels, 1)).astype(BF)
    flag = (iota((16, LANES), 1) == iota((16, LANES), 0) + LIVE).astype(F32).astype(BF)
    own_pack[half:] = jnp.zeros((16, LANES), BF)
    own_pack[half:, :local] = mm_nt(flag, own_tok[...]).astype(BF)

    def send_tok(i, how):
        h, dp, seq = chip_of(i)
        how(own_pack, tokp.at[slot * n_seq + j], TOK, dp, seq)

    each(send_tok)
    ring_step(0)
    each(send_text)
    back[...] = jnp.zeros_like(back)
    back[:, :channels] = mm_nt(xhat, embed[...])

    arrived(mods, MOD)
    tail = jnp.zeros((16, width), F32)
    at = iota((16, width), 0)
    for u in range(HALF):
        high, low = split(embed_centred * (1.0 + mods[u, 0]))
        amat[u * channels : (u + 1) * channels, :] = high
        amat[(HALF + u) * channels : (HALF + u + 1) * channels, :] = low
        high, low = split(mods[u, 1])
        tail = jnp.where(at == u, high.astype(F32), tail)
        tail = jnp.where(at == HALF + u, low.astype(F32), tail)
        high, low = split((1.0 + mods[u, 0]) * (1.0 / width))
        tail = jnp.where(at == 2 * HALF + u, high.astype(F32), tail)
        tail = jnp.where(at == 3 * HALF + u, low.astype(F32), tail)
    amat[2 * HALF * channels :, :] = tail.astype(BF)
    centred_b[...] = embed_centred.astype(BF)

    for step in range(1, last):
        ring_step(step)
    each(send_grad)

    arrived(tokp, TOK)
    half = local // 2
    low_lane = iota((half, LANES), 1) < channels
    for i in range(heads):
        packed = tokp[i, :half].astype(F32)
        flags = mm_tn(tokp[i, half:], flag)
        first = jnp.where(low_lane, packed, 0.0) + flags[:half]
        second = jnp.where(low_lane, pltpu.roll(packed, channels, 1), 0.0) + flags[half:local]
        tok[i * local : i * local + half] = first.astype(BF)
        tok[i * local + half : (i + 1) * local] = second.astype(BF)

    lane = iota((images, LANES), 1)
    tlane = iota((texts, LANES), 1)
    trow = iota((texts, LANES), 0)
    for u in range(HALF):
        tk = tok[u * images : (u + 1) * images]
        tf = tk.astype(F32)
        length = tf[0:1, TEXT_LEN : TEXT_LEN + 1]
        kaug[u, texts:, HD:] = jnp.where(lane == LIVE, (tf - 1.0) * 1e30, 0.0).astype(BF)
        bad = jnp.logical_and(tlane == LIVE, trow.astype(F32) >= length)
        kaug[u, :texts, HD:] = jnp.where(bad, -1e30, 0.0).astype(BF)
        vaug[u, :, HD:] = jnp.ones((total, LANES), BF)
        vt[u, HD:, :] = jnp.ones((16, total), BF)
        flag_rows = mm_nt(flag, tk)
        inv_row[u] = flag_rows[1:2] + flag_rows[2:3]
        scaled_t[u] = (tf.T * inv_row[u]).astype(BF)
        valid_row[u, :, texts:] = flag_rows[0:1]
        valid_row[u, :, :texts] = (iota((1, texts), 1).astype(F32) < length).astype(F32)
    arrived(qkv.at[:, pl.ds(0, texts), :], TXT)
    for u in range(HALF):
        kaug[u, :texts, :HD] = qkv[u, :texts, HD : 2 * HD]
        vaug[u, :texts, :HD] = qkv[u, :texts, 2 * HD :]
        kt[u, :, :texts] = qkv[u, :texts, HD : 2 * HD].T
        vt[u, :HD, :texts] = qkv[u, :texts, 2 * HD :].T

    ring_step(last)
    arrived(wbuf.at[pl.ds(0, n_z * HALF * rows), :], SIB)
    product = mm(amat[...], wbuf[...])
    base = 2 * HALF * channels
    for u in range(HALF):
        sums = (
            product[u * channels : (u + 1) * channels]
            + product[(HALF + u) * channels : (HALF + u + 1) * channels]
        )
        sums = jnp.concatenate([sums, jnp.zeros((LANES - channels, cols), F32)], axis=0)
        mixed[u, 0], mixed[u, 1] = split(sums)
        mixed_t[u, 0], mixed_t[u, 1] = split(sums.T)
        const = product[base + u : base + u + 1] + product[base + HALF + u : base + HALF + u + 1]
        wbar[u] = (
            product[base + 2 * HALF + u : base + 2 * HALF + u + 1]
            + product[base + 3 * HALF + u : base + 3 * HALF + u + 1]
        )
        const_t = jnp.broadcast_to(const[:, HD:], (LANES, 2 * HD)).T
        tk = tok[u * images : (u + 1) * images]
        tf = tk.astype(F32)
        invs = tf[:, INV_HIGH : INV_HIGH + 1] + tf[:, INV_LOW : INV_LOW + 1]
        got = ((mm(tk, mixed[u, 0]) + mm(tk, mixed[u, 1])) * invs + const).astype(BF)
        qkv[u, texts:, :HD] = got[:, :HD]
        kaug[u, texts:, :HD] = got[:, HD : 2 * HD]
        vaug[u, texts:, :HD] = got[:, 2 * HD :]
        got = mm_nt(mixed_t[u, 0, HD:], tk) + mm_nt(mixed_t[u, 1, HD:], tk)
        got = (got * inv_row[u] + const_t[:, 0:1]).astype(BF)
        kt[u, :, texts:] = got[:HD]
        vt[u, :HD, texts:] = got[HD:]

    factor = 1.0 / math.sqrt(HD)
    log2e = factor * math.log2(math.e)

    for u in range(HALF):
        query = qkv[u, :, :HD]
        ones = (iota((total, LANES), 1) == LIVE).astype(F32).astype(BF)
        score = mm_nt(kaug[u], jnp.concatenate([query, ones], axis=1))
        top = jnp.max(score, axis=0, keepdims=True)
        expo = jnp.exp2((score - top) * log2e).astype(BF)
        got = mm(vt[u], expo)
        share = valid_row[u] / got[HD : HD + 1]
        out_buf[u] = (got[:HD] * share).T.astype(BF)
        sbuf[u] = jnp.broadcast_to(share, (LANES, total)).T
        ebuf[u] = expo

    def slab(i):
        u = lax.rem(slot + lax.div(i, n_seq), HALF)
        return u, lax.rem(j + lax.rem(i, n_seq), n_seq)

    def send_out(i, how):
        u, s = slab(i)
        dp = z * Y + c * HALF + u
        rows_of = pl.ds(pl.multiple_of(texts + s * local, 16), local)
        how(out_buf.at[u, rows_of, :], img_recv.at[:, lanes(head, HD)], OIMG, dp, s)
        rows_of = pl.ds(pl.multiple_of(s * tloc, 16), tloc)
        how(out_buf.at[u, rows_of, :], txt_recv.at[:, lanes(head, HD)], OTXT, dp, s)

    each(send_out)

    arrived(dout.at[:, pl.ds(texts, images), :], DIMG)
    arrived(dout.at[:, pl.ds(0, texts), :], DTXT)
    lane = iota((total, LANES), 1)
    for u in range(HALF):
        expo, share = ebuf[u], sbuf[u]
        up = dout[u].astype(F32)
        delta = jnp.sum(up * out_buf[u].astype(F32), axis=1, keepdims=True) * share
        scaled = (up * share).astype(BF)
        high, low = split(delta)
        tail = jnp.where(lane == 0, -high.astype(F32), 0.0)
        tail = jnp.where(lane == 1, -low.astype(F32), tail).astype(BF)
        dprob = mm_nt(vaug[u], jnp.concatenate([scaled, tail], axis=1))
        dscore = expo * dprob.astype(BF)
        dqkv[u, :, 2 * HD :] = mm(expo, scaled).astype(BF)
        dqkv[u, :, HD : 2 * HD] = (mm(dscore, qkv[u, :, :HD]) * factor).astype(BF)
        dqkv[u, :, :HD] = (mm(kt[u], dscore) * factor).T.astype(BF)

    gram = jnp.zeros((LANES, LANES), F32)
    seen = []
    for u in range(HALF):
        grad = dqkv[u, texts:, :]
        seen.append(mm(scaled_t[u], grad)[:channels])
        scaled = scaled_t[u].astype(F32)
        project = jnp.sum(scaled * mm_nt(mixed[u, 0], grad), axis=0, keepdims=True)
        project = project * (inv_row[u] * (1.0 / width))
        gram += mm((scaled * project).astype(BF), tok[u * images : (u + 1) * images])
    seen = jnp.concatenate(seen, axis=0).astype(BF)
    gram = gram[:channels, :channels].astype(BF)
    average = jnp.zeros((channels, 1), F32)
    for u in range(HALF):
        mine = seen[u * channels : (u + 1) * channels].astype(F32)
        average += jnp.sum(mine * wbar[u], axis=1, keepdims=True)

    er, ec = channels // Y, width // n_seq

    me = y * n_seq + j
    plane = Y * n_seq

    def weight_block(i, carry):
        q = lax.rem(j + i, n_seq)
        at = lanes(q, ec)
        spread = mm_nt(seen, wbuf[pl.ds(pl.multiple_of(q * ec, LANES), ec), :])
        part = -mm(gram, centred_b[:, at]) - average
        for u in range(HALF):
            part += spread[u * channels : (u + 1) * channels] * (1.0 + mods[u, 0, :, at])
        for py in range(Y):
            t_send[py * n_seq + q] = part[py * er : (py + 1) * er].astype(BF)

            @pl.when(jnp.logical_not(jnp.logical_and(py == y, q == j)))
            def _():
                remote(t_send.at[py * n_seq + q], h1.at[me], H1, z * Y + py, q)

        return carry

    lax.fori_loop(0, n_seq, weight_block, 0)
    h1[me] = t_send[me]

    for u in range(HALF):
        part = mm(dqkv[u, texts:, :], mixed_t[u, 0])
        for s in range(n_seq):
            own_part = part[s * local : (s + 1) * local]
            packed = own_part[: local // 2] + pltpu.roll(own_part[local // 2 :], channels, 1)
            f_send[u * n_seq + s] = packed.astype(BF)

    def send_feat(i, how):
        u, s = slab(i)
        how(f_send.at[u * n_seq + s], f_recv.at[head], FEAT, z * Y + c * HALF + u, s)

    each(send_feat)

    arrived(h1.at[pl.ds(0, plane - 1)], H1)
    h2[z] = jnp.sum(h1[...].astype(F32), axis=0).astype(BF)

    def send_h2(i, carry):
        p = lax.rem(z + i, n_z)
        remote(h2.at[z], h2.at[z], H2, p * Y + y, j)
        return carry

    lax.fori_loop(1, n_z, send_h2, 0)
    arrived(f_recv, FEAT)
    half = local // 2
    packed = jnp.sum(f_recv[...].astype(F32), axis=0)
    lane = iota((half, LANES), 1)
    feat = jnp.concatenate(
        [
            jnp.where(lane < channels, packed, 0.0),
            jnp.where(lane < channels, pltpu.roll(packed, channels, 1), 0.0),
        ],
        axis=0,
    )
    mine = own_tok[...].astype(F32)
    inv = mine[:, INV_HIGH : INV_HIGH + 1] + mine[:, INV_LOW : INV_LOW + 1]
    project = jnp.sum(mine * feat, axis=1, keepdims=True) * (inv * (1.0 / width))
    ddeq = inv * (feat - back[...] * project)
    spread = mm_tn(gather, ddeq.astype(BF))
    for t in range(block):
        g_send[:, t, :] = spread[t * n_dp : (t + 1) * n_dp]

    def send_g(i, carry):
        p = lax.rem(d + i, n_dp)
        remote(g_send.at[p], g_recv.at[d], G, p, j)
        return carry

    lax.fori_loop(1, n_dp, send_g, 0)
    g_recv[d] = g_send[d]

    arrived(h2.at[pl.ds(0, n_z - 1)], H2)
    h3[me] = jnp.sum(h2[...].astype(F32), axis=0).astype(BF)

    def send_h3(i, carry):
        py, pj = plane_peer(i)

        @pl.when(i != Y // 2 * n_seq)
        def _():
            remote(h3.at[me], h3.at[me], H3, z * Y + py, pj)

        return carry

    lax.fori_loop(0, plane, send_h3, 0)

    arrived(img_recv, OIMG)
    arrived(txt_recv, OTXT)
    stores = [
        pltpu.make_async_copy(img_recv, out_img, store.at[0]),
        pltpu.make_async_copy(txt_recv, out_txt, store.at[1]),
    ]
    for copy in stores:
        copy.start()

    arrived(g_recv.at[pl.ds(0, n_dp - 1)], G)
    blocks = codes.shape[0]
    chosen = (slot_row[...] == iota((blocks, n_dp), 0)).astype(F32).astype(BF)
    pad_scale = mm(scales[...], pad_eye)
    codes_of = [mm(chosen, g_recv[:, t, :].astype(BF)) * pad_scale for t in range(block)]
    for t in range(0, block, 2):
        code_out[:, 0, t // 2 * LANES : (t // 2 + 1) * LANES] = codes_of[t] + pltpu.roll(
            codes_of[t + 1], channels, 1
        )

    left_here(a_send.at[pl.ds(0, n_dp - 1)], A)
    sent(weight.at[:, pl.ds(0, (HALF - 1) * cols)], weight.at[:, pl.ds(0, HALF * cols)], WY + slot)

    @pl.when(own)
    def _():
        for py in range(Y):

            @pl.when(py != y)
            def _():
                pltpu.make_async_copy(own_mods, own_mods, mod_send.at[py]).wait()

    few = heads - 1
    sent(text.at[:, pl.ds(0, few * cols)], text, TXT)
    sent(grad_txt.at[:, pl.ds(0, few * HD)], grad_txt, DTXT)
    sent(grad_img.at[:, pl.ds(0, few * HD)], grad_img, DIMG)
    sent(tokp.at[pl.ds(0, few)], tokp, TOK)
    left_here(wbuf.at[pl.ds(0, n_z * HALF * rows), :], SIB)
    gone = wbuf.at[pl.ds(0, (n_z - 1) * HALF * rows), :]
    pltpu.make_async_copy(gone, gone, ring_send).wait()
    sent(img_recv.at[:, pl.ds(0, few * HD)], img_recv, OIMG)
    sent(txt_recv.at[:, pl.ds(0, few * HD)], txt_recv, OTXT)
    sent(f_send.at[pl.ds(0, few)], f_send, FEAT)
    left_here(g_send.at[pl.ds(0, n_dp - 1)], G)
    left_here(h1.at[pl.ds(0, plane - 1)], H1)
    left_here(h2.at[pl.ds(0, n_z - 1)], H2)
    left_here(h1.at[pl.ds(0, plane - 1)], H3)

    arrived(h1.at[pl.ds(0, plane - 1)], H3)
    for py in range(Y):
        for q in range(n_seq):
            whole[py * er : (py + 1) * er, q * ec : (q + 1) * ec] = h3[py * n_seq + q]
    to_hbm = pltpu.make_async_copy(whole, embed_out, store.at[2])
    to_hbm.start()
    to_hbm.wait()
    for copy in stores:
        copy.wait()


def finish(*refs):
    sources, results, held = refs[:4], refs[4:8], refs[8:12]
    wide, came, went = refs[12:]
    inward = [
        pltpu.make_async_copy(sources[i], held[i], came.at[i]) for i in (3, 0, 1, 2)
    ]
    for copy in inward:
        copy.start()
    inward[0].wait()
    wide[...] = held[3][...].astype(F32)
    last = pltpu.make_async_copy(wide, results[3], went.at[3])
    last.start()
    outward = [pltpu.make_async_copy(held[i], results[i], went.at[i]) for i in range(3)]
    for before, copy in zip(inward[1:], outward):
        before.wait()
        copy.start()
    for copy in outward:
        copy.wait()
    last.wait()


def per_device(
    n_dp,
    n_seq,
    latent_codes,
    latent_scales,
    send_list,
    embed_weight,
    modulation_offset,
    mod_scale,
    qkv_weight,
    text_qkv,
    text_len,
    out_grad_img,
    out_grad_txt,
):
    codes, scales = latent_codes[0, 0], latent_scales[0, 0]
    slots = send_list[0, 0]
    channels, width = embed_weight.shape
    local, tloc = out_grad_img.shape[1], out_grad_txt.shape[1]
    images, texts = local * n_seq, tloc * n_seq
    total = images + texts
    heads = Y * n_seq // CORES
    cols = 3 * HD
    n_z = n_dp // Y
    er, ec = channels // Y, width // n_seq
    vmem, hbm = pl.BlockSpec(memory_space=pltpu.VMEM), pl.BlockSpec(memory_space=pltpu.HBM)
    block = codes.shape[1]
    scratch = [
        pltpu.SMEM((1,), jnp.int32),
        pltpu.VMEM(codes.shape, BF),
        pltpu.VMEM(scales.shape, BF),
        pltpu.VMEM((1, n_dp), jnp.int32),
        pltpu.VMEM((channels, width), BF),
        pltpu.VMEM((n_dp, 4, LANES), F32),
        pltpu.VMEM((n_dp, 4, LANES), F32),
        pltpu.VMEM((local, LANES), BF),
        pltpu.VMEM((local // 2 + 16, LANES), BF),
        pltpu.VMEM((heads, local // 2 + 16, LANES), BF),
        pltpu.VMEM((2, 1, width), F32),
        pltpu.VMEM((HALF * images, LANES), BF),
        pltpu.VMEM((HALF, 2, 1, width), F32),
        pltpu.VMEM((width, cols), BF),
        pltpu.VMEM((2 * HALF * channels + 16, width), BF),
        pltpu.VMEM((HALF, 2, LANES, cols), BF),
        pltpu.VMEM((HALF, total, cols), BF),
        pltpu.VMEM((HALF, total, HD), BF),
        pltpu.VMEM((HALF, total, 2 * HD), BF),
        pltpu.VMEM((HALF, total, 2 * HD), BF),
        pltpu.VMEM((HALF, HD, total), BF),
        pltpu.VMEM((HALF, HD + 16, total), BF),
        pltpu.VMEM((HALF, total, total), BF),
        pltpu.VMEM((HALF, total, LANES), F32),
        pltpu.VMEM((HALF, 2, cols, LANES), BF),
        pltpu.VMEM((HALF, 1, cols), F32),
        pltpu.VMEM((channels, width), BF),
        pltpu.VMEM((HALF, 1, images), F32),
        pltpu.VMEM((HALF, LANES, images), BF),
        pltpu.VMEM((HALF, 1, total), F32),
        pltpu.VMEM((HALF, total, HD), BF),
        pltpu.VMEM((local, heads * HD), BF),
        pltpu.VMEM((tloc, heads * HD), BF),
        pltpu.VMEM((HALF, total, cols), BF),
        pltpu.VMEM((heads, local // 2, LANES), BF),
        pltpu.VMEM((heads, local // 2, LANES), BF),
        pltpu.VMEM((local, LANES), F32),
        pltpu.VMEM((n_dp, 4, LANES), F32),
        pltpu.VMEM((n_dp, 4, LANES), F32),
        pltpu.VMEM((Y * n_seq, er, ec), BF),
        pltpu.VMEM((Y * n_seq, er, ec), BF),
        pltpu.VMEM((n_z, er, ec), BF),
        pltpu.VMEM((Y * n_seq, er, ec), BF),
        pltpu.VMEM((channels, width), BF),
        pltpu.SemaphoreType.DMA((7,)),
        pltpu.SemaphoreType.DMA((3,)),
        pltpu.SemaphoreType.DMA((16,)),
        pltpu.SemaphoreType.DMA((16,)),
        pltpu.SemaphoreType.DMA((Y,)),
        pltpu.SemaphoreType.DMA((n_z // 2, HALF)),
        pltpu.SemaphoreType.DMA((n_z // 2, HALF)),
        pltpu.SemaphoreType.DMA,
    ]
    out = pl.pallas_call(
        functools.partial(kernel, n_dp, n_seq),
        out_shape=(
            jax.ShapeDtypeStruct((local, heads * HD), BF),
            jax.ShapeDtypeStruct((tloc, heads * HD), BF),
            jax.ShapeDtypeStruct((codes.shape[0], 1, block), F32),
            jax.ShapeDtypeStruct((channels, width), BF),
        ),
        in_specs=[hbm] * 11,
        out_specs=(hbm, hbm, vmem, hbm),
        scratch_shapes=scratch,
        compiler_params=pltpu.CompilerParams(
            collective_id=0, has_side_effects=True, vmem_limit_bytes=61 * 1024 * 1024
        ),
    )(
        text_len,
        codes,
        scales,
        slots[None, :],
        embed_weight,
        modulation_offset,
        mod_scale,
        qkv_weight,
        text_qkv[0],
        out_grad_img[0],
        out_grad_txt[0],
    )
    img, txt, code, grad = pl.pallas_call(
        finish,
        out_shape=tuple(
            jax.ShapeDtypeStruct(part.shape, kind) for part, kind in zip(out, (BF, BF, F32, F32))
        ),
        in_specs=[hbm] * 4,
        out_specs=(hbm,) * 4,
        scratch_shapes=[pltpu.VMEM(part.shape, part.dtype) for part in out]
        + [
            pltpu.VMEM((channels, width), F32),
            pltpu.SemaphoreType.DMA((4,)),
            pltpu.SemaphoreType.DMA((4,)),
        ],
        compiler_params=pltpu.CompilerParams(vmem_limit_bytes=61 * 1024 * 1024),
    )(*out)
    return img[None], txt[None], code[:, 0][None, None], grad


def solution(mesh):
    return jax.shard_map(
        functools.partial(per_device, mesh.shape["dp"], mesh.shape["seq"]),
        mesh=mesh,
        in_specs=(
            P("dp", "seq", None, None),
            P("dp", "seq", None, None),
            P("dp", "seq", None),
            P(),
            P("dp", None),
            P("dp", None),
            P("dp", "seq"),
            P("dp", "seq", None),
            P("dp"),
            P("dp", "seq", None),
            P("dp", "seq", None),
        ),
        out_specs=(P("dp", "seq", None), P("dp", "seq", None), P("dp", "seq", None, None), P()),
        check_vma=False,
    )
```
